32 devices in a mesh: grp: 2 (over x), col: 16 (over z, y, core).
Axes of the slice: x: 2, y: 2, z: 4, core: 2. Of those that a mesh axis runs over, the one named last changes fastest.
Arguments:
- series: float32 [64, 8192], P(None, ('grp', 'col')), parts along dimension 1, as said below
- valid: int32 [64, 8192], P(None, ('grp', 'col')), parts along dimension 1, may hold values 0 or 1
- owners: int32 [8], P('grp'), parts along dimension 0, may hold values from 0 to 14, as said below
- blocks: int32 [8], P('grp'), parts along dimension 0, may hold values from 0 to 7, as said below
- excl: int32 [2], P('grp'), parts along dimension 0, may hold values from 32 to 256
Outputs:
- row_profile: float32 [8, 32], P('grp'), parts along dimension 0
- col_profile: float32 [8192], P(('grp', 'col')), parts along dimension 0
The draws below stay inside these ranges and needn't reach their ends.
There are 2 independent parts, one for each index of `grp`. The reference program is written for one: setup_inputs(seed, part) draws one part's arguments, and reference() takes and returns one part's arrays. A program takes and returns all parts, laid end to end along the dimension named above; each array names one. Nothing has to cross between parts.
Inputs may be any that keep to these rules, and one draw needn't show every extreme that they name: `series`: samples of smooth periodic components plus independent noise; every channel's noise has a standard deviation of at least 0.3 times the factor by which that channel's samples are multiplied. `owners`: the owner of a turn is never the last index of col. `blocks`: block of the owner's own starts.
All inputs are finite; a program needn't handle non-finite values. No bound on the sum of `valid` on one device may be relied on, other than what follows from the above.
Results may differ from the reference program's by a relative error of at most 0.00029.
Values sent between devices are 32-bit elements; how exact they have to be, the bound alone decides.
No kernel may reach another device: no remote copies, remote signals or barrier semaphores. Data moves between devices by JAX's collectives and lax.ppermute only.
A program may use at most 192 MiB of HBM per device.

```python
import math
import jax
import jax.numpy as jnp
from jax import lax

C = 64
M = 256
SEG = 256
QB = 32
TURNS = 4
COLS = 4096
N_COL = 16


def draw_series(key, part):
    keys = jax.random.split(key, 4)
    freq = jnp.exp(jax.random.uniform(keys[0], (C, 4), minval=math.log(1.0 / (16.0 * M)), maxval=math.log(2.0 / M)))
    ampl = jax.random.uniform(keys[1], (C, 4), minval=0.5, maxval=1.5)
    phase = jax.random.uniform(keys[2], (C, 4), minval=0.0, maxval=2.0 * math.pi)
    steps = jnp.arange(COLS, dtype=jnp.float32)
    cycles = jnp.mod(freq[:, :, None] * steps[None, None, :], 1.0)
    wave = jnp.sum(ampl[:, :, None] * jnp.sin(2.0 * math.pi * cycles + phase[:, :, None]), axis=1)
    noise = 0.35 * jax.random.normal(keys[3], (C, COLS))
    return (wave + noise).astype(jnp.float32)


def pinned_ints(key, count, upper):
    keys = jax.random.split(key, 3)
    values = jax.random.randint(keys[0], (count,), 0, upper + 1)
    high_at = jax.random.randint(keys[1], (), 0, count)
    low_at = (high_at + 1 + jax.random.randint(keys[2], (), 0, count - 1)) % count
    steps = jnp.arange(count)
    values = jnp.where(steps == high_at, upper, values)
    values = jnp.where(steps == low_at, 0, values)
    return values.astype(jnp.int32)


def draw_owners(key, part):
    return pinned_ints(jax.random.fold_in(key, 11), TURNS, N_COL - 2)


def draw_blocks(key, part):
    return pinned_ints(jax.random.fold_in(key, 23), TURNS, SEG // QB - 1)


def plant(values, stream_key, least, largest):
    shape = values.shape
    index_at = [jax.random.randint(jax.random.fold_in(stream_key, axis), (), 0, shape[axis]) for axis in range(len(shape))]
    values = values.at[tuple(index_at)].set(least)
    longest = shape.index(max(shape))
    index_at[longest] = (index_at[longest] + 1) % shape[longest]
    return values.at[tuple(index_at)].set(largest)


def setup_inputs(seed: int = 0, part: int = 0) -> dict:
    key_of = jax.random.split(jax.random.key(seed), 6)
    own_keys = jax.random.split(jax.random.fold_in(key_of[5], part), 6)
    series = draw_series(jax.random.fold_in(jax.random.fold_in(key_of[5], part), 71), part)
    valid = plant((jax.random.randint(own_keys[1], (C, COLS), 0, 8) < 7).astype(jnp.int32), jax.random.fold_in(own_keys[1], 1), 0, 1)
    owners = draw_owners(jax.random.fold_in(jax.random.fold_in(key_of[5], part), 71), part)
    blocks = draw_blocks(jax.random.fold_in(jax.random.fold_in(key_of[5], part), 71), part)
    excl = jax.random.randint(own_keys[4], (1,), M // 8, M + 1).astype(jnp.int32)
    return dict(series=series, valid=valid, owners=owners, blocks=blocks, excl=excl)


highest = lax.Precision.HIGHEST

def slide(signal, kernels, groups):
    return lax.conv_general_dilated(signal[None], kernels, (1,), 'VALID', feature_group_count=groups, precision=highest)[0]

def window_stats(extended, valid, count):
    channels = extended.shape[0]
    ones_kernel = jnp.ones((channels, 1, M), jnp.float32)
    first = slide(extended, ones_kernel, channels)[:, :count]
    second = slide(extended * extended, ones_kernel, channels)[:, :count]
    mean_all = first / M
    spread = second / M - mean_all * mean_all
    scale_all = valid.astype(jnp.float32) / jnp.sqrt(spread + 1e-05)
    return (mean_all, scale_all)

def turn_profile(extended, mean_all, scale_all, samples, q_mean, q_scale, count):
    channels = extended.shape[0]
    offsets = jnp.arange(QB)[:, None] + jnp.arange(M)[None, :]
    windows = samples[:, offsets]
    summed = jnp.zeros((QB, count), jnp.float32)
    for group in range(channels // 8):
        first_ch = group * 8
        kernels = windows[first_ch:first_ch + 8].reshape(8 * QB, 1, M)
        products = slide(extended[first_ch:first_ch + 8], kernels, 8).reshape(8, QB, -1)[:, :, :count]
        centred = products - M * q_mean[first_ch:first_ch + 8, :, None] * mean_all[first_ch:first_ch + 8, None, :]
        summed = summed + lax.optimization_barrier(jnp.sum(centred * q_scale[first_ch:first_ch + 8, :, None] * scale_all[first_ch:first_ch + 8, None, :], axis=0))
    return 1.0 - summed / (M * channels)

def exclude(profile, queries, columns, excl, limit):
    banned = (jnp.abs(queries[:, None] - columns[None, :]) < excl[0]) | (columns > limit)[None, :]
    return jnp.where(banned, jnp.float32(4.0), profile)

def reference(series, valid, owners, blocks, excl):
    channels, total = series.shape
    padded = jnp.pad(series, ((0, 0), (0, M - 1)))
    mean_all, scale_all = window_stats(padded, valid, total)
    columns = jnp.arange(total, dtype=jnp.int32)
    column_min = jnp.full((total,), 4.0, jnp.float32)
    zero = jnp.zeros((), jnp.int32)
    rows_out = []
    for turn in range(owners.shape[0]):
        start = (owners[turn] * SEG + blocks[turn] * QB).astype(jnp.int32)
        samples = lax.dynamic_slice(padded, (zero, start), (channels, QB + M - 1))
        q_mean = lax.dynamic_slice(mean_all, (zero, start), (channels, QB))
        q_scale = lax.dynamic_slice(scale_all, (zero, start), (channels, QB))
        profile = turn_profile(padded, mean_all, scale_all, samples, q_mean, q_scale, total)
        queries = start + jnp.arange(QB, dtype=jnp.int32)
        profile = exclude(profile, queries, columns, excl, total - M)
        column_min = jnp.minimum(column_min, lax.optimization_barrier(jnp.min(profile, axis=0)))
        rows_out.append(lax.optimization_barrier(jnp.min(profile, axis=1)))
    col_profile = jnp.where(columns > total - M, jnp.float32(0.0), column_min)
    return (jnp.stack(rows_out), col_profile)
```

```python
import functools

import jax
import jax.numpy as jnp
from jax import lax
from jax.experimental import pallas as pl
from jax.experimental.pallas import tpu as pltpu
from jax.sharding import PartitionSpec as P

M = 256
QB = 32
GROUP = 4
LANES = 128

f32 = jnp.float32
bf16 = jnp.bfloat16


def exchanged(block, mask):
    devices = range(lax.axis_size("col"))
    return lax.ppermute(block, "col", [(i, i ^ mask) for i in devices])


def rounds_beyond_group(devices):
    rounds, base, left = [], GROUP, devices // GROUP
    while left > 1:
        radix = 4 if left % 4 == 0 else 2
        rounds.append([base * i for i in range(1, radix)])
        base, left = base * radix, left // radix
    return rounds


def split3(value):
    high = value.astype(bf16)
    rest = value - high.astype(f32)
    mid = rest.astype(bf16)
    low = (rest - mid.astype(f32)).astype(bf16)
    return high, mid, low


def contributions_kernel(owners, blocks, x_ref, v_ref, *outs):
    turns = owners.shape[0]
    quarter = x_ref.shape[0] // GROUP
    width = x_ref.shape[1]
    here = lax.axis_index("col")
    member = lax.rem(here, GROUP)
    row = lax.broadcasted_iota(jnp.int32, (width, width), 0)
    col = lax.broadcasted_iota(jnp.int32, (width, width), 1)
    flip = (row + col == width - 1).astype(bf16)
    lane = lax.broadcasted_iota(jnp.int32, (quarter, width), 1)
    lane_128 = lax.broadcasted_iota(jnp.int32, (quarter, LANES), 1)
    per_tile = LANES // QB
    for mask, out in enumerate(outs):
        rows = pl.ds(pl.multiple_of((member ^ mask) * quarter, quarter), quarter)
        pieces = split3(x_ref[rows, :])
        turned = sum(jnp.dot(p, flip, preferred_element_type=f32) for p in reversed(pieces))
        flags = v_ref[rows, :].astype(f32)
        for tile in range(turns // per_tile):
            tails = jnp.zeros((quarter, LANES), f32)
            valids = jnp.zeros((quarter, LANES), f32)
            for i in range(per_tile):
                turn = tile * per_tile + i
                shift = blocks[turn] * QB
                mine = owners[turn] == here
                after = owners[turn] + 1 == here
                rolled = pltpu.roll(turned, lax.rem(shift + QB, width), 1)
                split = shift + QB
                keep = jnp.where(lane >= split, mine.astype(jnp.int32), after.astype(jnp.int32)) == 1
                out[:, turn * M : (turn + 1) * M] = jnp.where(keep, rolled, 0.0)
                there = (lane_128 >= i * QB) & (lane_128 < (i + 1) * QB) & (mine.astype(jnp.int32) == 1)
                tail = rolled[:, :LANES]
                flag = pltpu.roll(flags, lax.rem(width - shift, width), 1)[:, :LANES]
                if i:
                    tail = pltpu.roll(tail, i * QB, 1)
                    flag = pltpu.roll(flag, i * QB, 1)
                tails = jnp.where(there, tail, tails)
                valids = jnp.where(there, flag, valids)
            at = turns * M + tile * LANES
            out[:, at : at + LANES] = tails
            at = turns * (M + QB) + tile * LANES
            out[:, at : at + LANES] = valids


def query_kernel(turns, band_ref, *refs):
    parts, out = refs[:-1], refs[-1]
    total = parts[0][...]
    for part in parts[1:]:
        total = total + part[...]
    samples = turns * (M + QB)
    per_tile = LANES // QB
    main, tail = [], []
    for tile in range(turns // per_tile):
        at = turns * M + tile * LANES
        tail_tile = total[:, at : at + LANES]
        lane = lax.broadcasted_iota(jnp.int32, tail_tile.shape, 1)
        centre = jnp.zeros_like(tail_tile)
        for i in range(per_tile):
            turn = tile * per_tile + i
            block = total[:, turn * M : (turn + 1) * M]
            mean = jnp.sum(block, axis=1, keepdims=True) * (1.0 / M)
            main.append(block - mean)
            centre = jnp.where((lane >= i * QB) & (lane < (i + 1) * QB), mean, centre)
        tail.append(tail_tile - centre)
    for tile in range(turns // per_tile):
        rows = main[tile * per_tile : (tile + 1) * per_tile] + [tail[tile]]
        shifted = jnp.concatenate(rows, axis=1)
        quarter = shifted.shape[0]
        stack = jnp.concatenate([*split3(shifted), *split3(shifted * shifted)], axis=0)
        sums = jnp.dot(stack, band_ref[...], preferred_element_type=f32)
        first = sums[2 * quarter : 3 * quarter] + sums[quarter : 2 * quarter] + sums[:quarter]
        second = sums[5 * quarter : 6 * quarter] + sums[4 * quarter : 5 * quarter] + sums[3 * quarter : 4 * quarter]
        mean = first * (1.0 / M)
        spread = second * (1.0 / M) - mean * mean
        at = samples + tile * LANES
        scale = total[:, at : at + LANES] / jnp.sqrt(spread + 1e-05)
        out[:, at : at + LANES] = scale
        out[:, at + turns * QB : at + turns * QB + LANES] = mean * scale
    for turn in range(turns):
        out[:, turn * M : (turn + 1) * M] = main[turn]
    for tile in range(turns // per_tile):
        at = turns * M + tile * LANES
        out[:, at : at + LANES] = tail[tile]


def band_matrix():
    per_tile = LANES // QB
    query = jnp.arange(LANES)
    lane = jnp.arange(per_tile * (M + QB))
    in_main = lane < per_tile * M
    turn = jnp.where(in_main, lane // M, (lane - per_tile * M) // QB)
    place = jnp.where(in_main, lane % M, M + (lane - per_tile * M) % QB)
    q = query % QB
    inside = (place[:, None] >= QB - q[None, :]) & (place[:, None] <= M + QB - 1 - q[None, :])
    return ((turn[:, None] == query[None, :] // QB) & inside).astype(bf16)


def columns_kernel(first_mask, x_ref, h_ref, v_ref, hankel, scale_ref, offset_ref):
    quarter = x_ref.shape[0] // GROUP
    width = x_ref.shape[1]
    member = lax.rem(lax.axis_index("col"), GROUP)
    for piece in range(2):
        rows = pl.ds(pl.multiple_of((member ^ (first_mask + piece)) * quarter, quarter), quarter)
        own = x_ref[rows, :]
        centre = jnp.sum(own, axis=1, keepdims=True) * (1.0 / width)
        extended = jnp.concatenate([own - centre, h_ref[rows, :] - centre], axis=1)
        length = extended.shape[1]
        first, second = extended, extended * extended
        step = 1
        while step < M:
            first = first + pltpu.roll(first, length - step, 1)
            second = second + pltpu.roll(second, length - step, 1)
            step *= 2
        mean = first[:, :width] * (1.0 / M)
        spread = second[:, :width] * (1.0 / M) - mean * mean
        scale = v_ref[rows, :].astype(f32) / jnp.sqrt(jnp.maximum(spread, 0.0) + 1e-05)
        into = slice(piece * quarter, (piece + 1) * quarter)
        scale_ref[into, :] = scale
        offset_ref[into, :] = mean * scale
        for c in range(quarter):
            base = jnp.broadcast_to(extended[c : c + 1, :], (16, length))
            base = pltpu.roll(base, length - 15, 1, stride=1, stride_axis=0).astype(bf16)
            for b in range(M // 16):
                shift = M - 16 - 16 * b
                block = pltpu.roll(base, length - shift, 1) if shift else base
                hankel[piece * quarter + c, 16 * b : 16 * (b + 1), :] = block[:, :width]


def partial_sum(turns, pieces, hankel, scale_ref, offset_ref, acc):
    queries = turns * QB
    samples = turns * (M + QB)
    per_tile = LANES // QB
    quarter = pieces[0].shape[0]
    for index, piece in enumerate(pieces):
        by_query = jnp.transpose(piece[:, samples : samples + queries])
        offsets = jnp.transpose(piece[:, samples + queries : samples + 2 * queries])
        lines = []
        for turn in range(turns):
            at = turns * M + (turn // per_tile) * LANES
            tail = piece[:, at : at + LANES]
            if turn % per_tile:
                tail = pltpu.roll(tail, LANES - (turn % per_tile) * QB, 1)
            lines.append(jnp.concatenate([piece[:, turn * M : (turn + 1) * M], tail], axis=1))
        length = M + LANES
        for c in range(quarter):
            windows = []
            for turn in range(turns):
                row = jnp.broadcast_to(lines[turn][c : c + 1, :], (QB, length))
                row = pltpu.roll(row, length - QB, 1, stride=1, stride_axis=0)
                windows.append(row[:, :M].astype(bf16))
            at = index * quarter + c
            products = jnp.dot(jnp.concatenate(windows, axis=0), hankel[at], preferred_element_type=f32)
            acc = acc + products * by_query[:, c : c + 1] * scale_ref[at : at + 1, :]
        rows = slice(index * quarter, (index + 1) * quarter)
        means = jnp.dot(offsets, offset_ref[rows, :], preferred_element_type=f32, precision=lax.Precision.HIGHEST)
        acc = acc - M * means
    return acc


def first_half_kernel(turns, ya, yb, hankel, scale_ref, offset_ref, out):
    zero = jnp.zeros(out.shape, f32)
    out[...] = partial_sum(turns, (ya, yb), hankel, scale_ref, offset_ref, zero)


def second_half_kernel(
    turns, channels, limit, owners, blocks, excl, ya, yb, hankel, scale_ref, offset_ref, so_far, row_out, col_out
):
    summed = partial_sum(turns, (ya, yb), hankel, scale_ref, offset_ref, so_far[...])
    distance = 1.0 - summed * (1.0 / (M * channels))
    width = distance.shape[1]
    columns = lax.axis_index("col") * width + lax.broadcasted_iota(jnp.int32, (QB, width), 1)
    within = lax.broadcasted_iota(jnp.int32, (QB, width), 0)
    beyond = columns > limit
    column_min = jnp.full((1, width), 4.0, f32)
    rows = []
    for turn in range(turns):
        query = owners[turn] * width + blocks[turn] * QB + within
        banned = (jnp.abs(query - columns) < excl[0]) | beyond
        block = jnp.where(banned, 4.0, distance[turn * QB : (turn + 1) * QB, :])
        column_min = jnp.minimum(column_min, jnp.min(block, axis=0, keepdims=True))
        rows.append(jnp.min(block, axis=1, keepdims=True))
    col_out[...] = jnp.where(beyond[:1, :], 0.0, column_min)
    stacked = jnp.concatenate(rows, axis=0)
    flat = jnp.transpose(jnp.broadcast_to(stacked, (turns * QB, LANES)))[:1, :]
    for turn in range(turns):
        row_out[turn : turn + 1, :] = flat[:, turn * QB : (turn + 1) * QB]


VMEM = pl.BlockSpec(memory_space=pltpu.VMEM)
SMEM = pl.BlockSpec(memory_space=pltpu.SMEM)
PARAMS = pltpu.CompilerParams(vmem_limit_bytes=40 * 2**20)


def shards(series, valid, owners, blocks, excl):
    channels, seg_len = series.shape
    devices_col = lax.axis_size("col")
    turns = owners.shape[0]
    quarter = channels // GROUP
    queries = turns * QB
    limit = seg_len * devices_col - M

    following = lax.ppermute(series, "col", [(i, i - 1) for i in range(1, devices_col)])

    share = jax.ShapeDtypeStruct((quarter, turns * (M + 2 * QB)), f32)
    shares = pl.pallas_call(
        contributions_kernel,
        out_shape=[share] * GROUP,
        in_specs=[SMEM, SMEM, VMEM, VMEM],
        out_specs=[VMEM] * GROUP,
        compiler_params=PARAMS,
        name="contributions",
    )(owners, blocks, series, valid)
    arrived = [exchanged(shares[mask], mask) for mask in (3, 2, 1)]
    total = shares[0] + arrived[0] + arrived[1] + arrived[2]

    rounds = rounds_beyond_group(devices_col)
    for masks in rounds[:-1]:
        total = sum([exchanged(total, mask) for mask in masks], total)
    order = (0, 2, 1) if len(rounds[-1]) == 3 else (0,)
    parts = [total] + [exchanged(total, rounds[-1][i]) for i in order]
    query = jax.ShapeDtypeStruct((quarter, turns * (M + 3 * QB)), f32)
    mine = pl.pallas_call(
        functools.partial(query_kernel, turns),
        out_shape=query,
        in_specs=[VMEM] * (1 + len(parts)),
        out_specs=VMEM,
        compiler_params=PARAMS,
        name="query_stats",
    )(band_matrix(), *parts)

    def column_side(first_mask):
        return pl.pallas_call(
            functools.partial(columns_kernel, first_mask),
            out_shape=[
                jax.ShapeDtypeStruct((2 * quarter, M, seg_len), bf16),
                jax.ShapeDtypeStruct((2 * quarter, seg_len), f32),
                jax.ShapeDtypeStruct((2 * quarter, seg_len), f32),
            ],
            in_specs=[VMEM] * 3,
            out_specs=[VMEM] * 3,
            compiler_params=PARAMS,
            cost_estimate=pl.CostEstimate(flops=10**8, bytes_accessed=8 * 2**20, transcendentals=0),
            name="columns",
        )(series, following, valid)

    sides = column_side(0), column_side(2)
    others = {mask: exchanged(mine, mask) for mask in (3, 2, 1)}

    half = pl.pallas_call(
        functools.partial(first_half_kernel, turns),
        out_shape=jax.ShapeDtypeStruct((queries, seg_len), f32),
        in_specs=[VMEM] * 5,
        out_specs=VMEM,
        compiler_params=PARAMS,
        cost_estimate=pl.CostEstimate(flops=5 * 10**8, bytes_accessed=4 * 2**20, transcendentals=0),
        name="first_half",
    )(mine, others[1], *sides[0])
    rows, column = pl.pallas_call(
        functools.partial(second_half_kernel, turns, channels, limit),
        out_shape=[jax.ShapeDtypeStruct((turns, QB), f32), jax.ShapeDtypeStruct((1, seg_len), f32)],
        in_specs=[SMEM] * 3 + [VMEM] * 6,
        out_specs=[VMEM] * 2,
        compiler_params=PARAMS,
        name="second_half",
    )(owners, blocks, excl, others[2], others[3], *sides[1], half)

    for masks in [[1, 2, 3], *rounds]:
        rows = functools.reduce(jnp.minimum, [exchanged(rows, mask) for mask in masks], rows)
    return (rows, column.reshape(seg_len))


def solution(mesh):
    return jax.shard_map(
        shards,
        mesh=mesh,
        in_specs=(P(None, ("grp", "col")), P(None, ("grp", "col")), P("grp"), P("grp"), P("grp")),
        out_specs=(P("grp", None), P(("grp", "col"))),
        check_vma=False,
    )
```

```python
import functools

import jax
import jax.numpy as jnp
from jax import lax
from jax.experimental import pallas as pl
from jax.experimental.pallas import tpu as pltpu
from jax.sharding import PartitionSpec as P

M = 256
QB = 32
GROUP = 4
LANES = 128

f32 = jnp.float32
bf16 = jnp.bfloat16


def exchanged(block, mask):
    devices = range(lax.axis_size("col"))
    return lax.ppermute(block, "col", [(i, i ^ mask) for i in devices])


def rounds_beyond_group(devices):
    rounds, base, left = [], GROUP, devices // GROUP
    while left > 1:
        radix = 4 if left % 4 == 0 else 2
        rounds.append([base * i for i in range(1, radix)])
        base, left = base * radix, left // radix
    return rounds


def split3(value):
    high = value.astype(bf16)
    rest = value - high.astype(f32)
    mid = rest.astype(bf16)
    low = (rest - mid.astype(f32)).astype(bf16)
    return high, mid, low


def share_kernel(packed, samples, flags, *outs):
    width = samples.shape[1]
    quarter = packed.shape[0] // GROUP
    member = lax.rem(lax.axis_index("col"), GROUP)
    samples[...] = packed[:, :width]
    flags[...] = packed[:, width:]
    for mask, out in enumerate(outs):
        out[...] = packed[pl.ds(pl.multiple_of((member ^ mask) * quarter, quarter), quarter), :]


def windows_kernel(owners, blocks, after, *refs):
    parts, out = refs[:GROUP], refs[GROUP]
    turns = owners.shape[0]
    quarter, width = parts[0].shape[0], parts[0].shape[1] // 2
    here = lax.axis_index("col")
    row = lax.broadcasted_iota(jnp.int32, (width, width), 0)
    col = lax.broadcasted_iota(jnp.int32, (width, width), 1)
    flip = (row + col == width - 1).astype(bf16)
    stack = jnp.concatenate([piece for part in parts for piece in split3(part[:, :width])], axis=0)
    turned = jnp.dot(stack, flip, preferred_element_type=f32)
    lines = []
    for i in range(GROUP):
        high, mid, low = (turned[(3 * i + j) * quarter : (3 * i + j + 1) * quarter] for j in range(3))
        lines.append(low + mid + high)
    lane = lax.broadcasted_iota(jnp.int32, (quarter, width), 1)
    lane_128 = lax.broadcasted_iota(jnp.int32, (quarter, LANES), 1)
    per_tile = LANES // QB
    for tile in range(turns // per_tile):
        tails = jnp.zeros((quarter, LANES), f32)
        valids = jnp.zeros((quarter, LANES), f32)
        for i in range(per_tile):
            turn = tile * per_tile + i
            shift = blocks[turn] * QB
            split = shift + QB
            first = jnp.zeros((quarter, width), f32)
            second = jnp.zeros((quarter, width), f32)
            flags = jnp.zeros((quarter, width), f32)
            for mask, part in enumerate(parts):
                mine = (owners[turn] == here ^ mask).astype(f32)
                after_mine = (owners[turn] + 1 == here ^ mask).astype(f32)
                first = first + mine * lines[mask]
                second = second + after_mine * lines[mask]
                flags = flags + mine * part[:, width:]
            amount = lax.rem(split, width)
            first = pltpu.roll(first, amount, 1)
            second = pltpu.roll(second, amount, 1)
            flags = pltpu.roll(flags, lax.rem(width - shift, width), 1)
            out[:, turn * M : (turn + 1) * M] = jnp.where(lane >= split, first, second)
            tail, flag = first[:, :LANES], flags[:, :LANES]
            if i:
                tail = pltpu.roll(tail, i * QB, 1)
                flag = pltpu.roll(flag, i * QB, 1)
            there = (lane_128 >= i * QB) & (lane_128 < (i + 1) * QB)
            tails = jnp.where(there, tail, tails)
            valids = jnp.where(there, flag, valids)
        at = turns * M + tile * LANES
        out[:, at : at + LANES] = tails
        at = turns * (M + QB) + tile * LANES
        out[:, at : at + LANES] = valids


def query_kernel(turns, after, band_ref, *refs):
    parts, out = refs[:-1], refs[-1]
    total = parts[0][...]
    for part in parts[1:]:
        total = total + part[...]
    samples = turns * (M + QB)
    per_tile = LANES // QB
    main, tail = [], []
    for tile in range(turns // per_tile):
        at = turns * M + tile * LANES
        tail_tile = total[:, at : at + LANES]
        lane = lax.broadcasted_iota(jnp.int32, tail_tile.shape, 1)
        centre = jnp.zeros_like(tail_tile)
        for i in range(per_tile):
            turn = tile * per_tile + i
            block = total[:, turn * M : (turn + 1) * M]
            mean = jnp.sum(block, axis=1, keepdims=True) * (1.0 / M)
            main.append(block - mean)
            centre = jnp.where((lane >= i * QB) & (lane < (i + 1) * QB), mean, centre)
        tail.append(tail_tile - centre)
    for tile in range(turns // per_tile):
        rows = main[tile * per_tile : (tile + 1) * per_tile] + [tail[tile]]
        shifted = jnp.concatenate(rows, axis=1)
        quarter = shifted.shape[0]
        stack = jnp.concatenate([*split3(shifted), *split3(shifted * shifted)], axis=0)
        sums = jnp.dot(stack, band_ref[...], preferred_element_type=f32)
        first = sums[2 * quarter : 3 * quarter] + sums[quarter : 2 * quarter] + sums[:quarter]
        second = sums[5 * quarter : 6 * quarter] + sums[4 * quarter : 5 * quarter] + sums[3 * quarter : 4 * quarter]
        mean = first * (1.0 / M)
        spread = second * (1.0 / M) - mean * mean
        at = samples + tile * LANES
        scale = total[:, at : at + LANES] / jnp.sqrt(spread + 1e-05)
        out[:, at : at + LANES] = scale
        out[:, at + turns * QB : at + turns * QB + LANES] = mean * scale
    for turn in range(turns):
        out[:, turn * M : (turn + 1) * M] = main[turn]
    for tile in range(turns // per_tile):
        at = turns * M + tile * LANES
        out[:, at : at + LANES] = tail[tile]


def band_matrix(shape):
    lane = lax.broadcasted_iota(jnp.int32, shape, 0)
    query = lax.broadcasted_iota(jnp.int32, shape, 1)
    per_tile = LANES // QB
    beyond = lane - per_tile * M
    turn = jnp.where(beyond < 0, lane // M, beyond // QB)
    place = jnp.where(beyond < 0, lane % M, M + beyond % QB)
    q = query % QB
    inside = (turn == query // QB) & (place >= QB - q) & (place <= M + QB - 1 - q)
    return jnp.where(inside, 1.0, 0.0).astype(bf16)


def columns_kernel(first_mask, x_ref, h_ref, v_ref, hankel, scale_ref, offset_ref, *band_ref):
    quarter = x_ref.shape[0] // GROUP
    width = x_ref.shape[1]
    member = lax.rem(lax.axis_index("col"), GROUP)
    for ref in band_ref:
        ref[...] = band_matrix(ref.shape)
    for piece in range(2):
        rows = pl.ds(pl.multiple_of((member ^ (first_mask + piece)) * quarter, quarter), quarter)
        own = x_ref[rows, :]
        centre = jnp.sum(own, axis=1, keepdims=True) * (1.0 / width)
        extended = jnp.concatenate([own - centre, h_ref[rows, :] - centre], axis=1)
        length = extended.shape[1]
        first, second = extended, extended * extended
        step = 1
        while step < M:
            first = first + pltpu.roll(first, length - step, 1)
            second = second + pltpu.roll(second, length - step, 1)
            step *= 2
        mean = first[:, :width] * (1.0 / M)
        spread = second[:, :width] * (1.0 / M) - mean * mean
        scale = v_ref[rows, :] / jnp.sqrt(jnp.maximum(spread, 0.0) + 1e-05)
        into = slice(piece * quarter, (piece + 1) * quarter)
        scale_ref[into, :] = scale
        offset_ref[into, :] = mean * scale
        for c in range(quarter):
            base = jnp.broadcast_to(extended[c : c + 1, :], (16, length))
            base = pltpu.roll(base, length - 15, 1, stride=1, stride_axis=0).astype(bf16)
            for b in range(M // 16):
                shift = M - 16 - 16 * b
                block = pltpu.roll(base, length - shift, 1) if shift else base
                hankel[piece * quarter + c, 16 * b : 16 * (b + 1), :] = block[:, :width]


def partial_sum(turns, pieces, held_at, hankel, scale_ref, offset_ref, acc):
    queries = turns * QB
    samples = turns * (M + QB)
    per_tile = LANES // QB
    quarter = pieces[0].shape[0]
    for index, piece in enumerate(pieces, held_at):
        by_query = jnp.transpose(piece[:, samples : samples + queries])
        offsets = jnp.transpose(piece[:, samples + queries : samples + 2 * queries])
        lines = []
        for turn in range(turns):
            at = turns * M + (turn // per_tile) * LANES
            tail = piece[:, at : at + LANES]
            if turn % per_tile:
                tail = pltpu.roll(tail, LANES - (turn % per_tile) * QB, 1)
            lines.append(jnp.concatenate([piece[:, turn * M : (turn + 1) * M], tail], axis=1))
        length = M + LANES
        for c in range(quarter):
            windows = []
            for turn in range(turns):
                row = jnp.broadcast_to(lines[turn][c : c + 1, :], (QB, length))
                row = pltpu.roll(row, length - QB, 1, stride=1, stride_axis=0)
                windows.append(row[:, :M].astype(bf16))
            at = index * quarter + c
            products = jnp.dot(jnp.concatenate(windows, axis=0), hankel[at], preferred_element_type=f32)
            acc = acc + products * by_query[:, c : c + 1] * scale_ref[at : at + 1, :]
        rows = slice(index * quarter, (index + 1) * quarter)
        means = jnp.dot(offsets, offset_ref[rows, :], preferred_element_type=f32, precision=lax.Precision.HIGHEST)
        acc = acc - M * means
    return acc


def first_kernel(turns, ya, yb, hankel, scale_ref, offset_ref, out):
    zero = jnp.zeros(out.shape, f32)
    out[...] = partial_sum(turns, (ya, yb), 0, hankel, scale_ref, offset_ref, zero)


def next_kernel(turns, y, hankel, scale_ref, offset_ref, so_far, out):
    out[...] = partial_sum(turns, (y,), 0, hankel, scale_ref, offset_ref, so_far[...])


def last_kernel(
    turns, channels, limit, owners, blocks, excl, y, hankel, scale_ref, offset_ref, so_far, row_out, col_out
):
    summed = partial_sum(turns, (y,), 1, hankel, scale_ref, offset_ref, so_far[...])
    distance = 1.0 - summed * (1.0 / (M * channels))
    width = distance.shape[1]
    columns = lax.axis_index("col") * width + lax.broadcasted_iota(jnp.int32, (QB, width), 1)
    within = lax.broadcasted_iota(jnp.int32, (QB, width), 0)
    beyond = columns > limit
    column_min = jnp.full((1, width), 4.0, f32)
    rows = []
    for turn in range(turns):
        query = owners[turn] * width + blocks[turn] * QB + within
        banned = (jnp.abs(query - columns) < excl[0]) | beyond
        block = jnp.where(banned, 4.0, distance[turn * QB : (turn + 1) * QB, :])
        column_min = jnp.minimum(column_min, jnp.min(block, axis=0, keepdims=True))
        rows.append(jnp.min(block, axis=1, keepdims=True))
    col_out[...] = jnp.where(beyond[:1, :], 0.0, column_min)
    stacked = jnp.concatenate(rows, axis=0)
    flat = jnp.transpose(jnp.broadcast_to(stacked, (turns * QB, LANES)))[:1, :]
    for turn in range(turns):
        row_out[turn : turn + 1, :] = flat[:, turn * QB : (turn + 1) * QB]


VMEM = pl.BlockSpec(memory_space=pltpu.VMEM)
SMEM = pl.BlockSpec(memory_space=pltpu.SMEM)
ANY = pl.BlockSpec(memory_space=pl.ANY)
PARAMS = pltpu.CompilerParams(vmem_limit_bytes=40 * 2**20)


def shards(series, valid, owners, blocks, excl):
    channels, seg_len = series.shape
    devices_col = lax.axis_size("col")
    turns = owners.shape[0]
    quarter = channels // GROUP
    queries = turns * QB
    limit = seg_len * devices_col - M

    packed = jnp.concatenate([series, valid.astype(f32)], axis=1)
    segment = jax.ShapeDtypeStruct(series.shape, f32)
    part = jax.ShapeDtypeStruct((quarter, 2 * seg_len), f32)
    samples, flags, *shares = pl.pallas_call(
        share_kernel,
        out_shape=[segment] * 2 + [part] * GROUP,
        in_specs=[VMEM],
        out_specs=[VMEM] * (2 + GROUP),
        compiler_params=PARAMS,
        name="share",
    )(packed)
    arrived = {mask: exchanged(shares[mask], mask) for mask in (3, 2, 1)}
    following = lax.ppermute(samples, "col", [(i, i - 1) for i in range(1, devices_col)])

    def column_side(first_mask, *band):
        return pl.pallas_call(
            functools.partial(columns_kernel, first_mask),
            out_shape=[
                jax.ShapeDtypeStruct((2 * quarter, M, seg_len), bf16),
                jax.ShapeDtypeStruct((2 * quarter, seg_len), f32),
                jax.ShapeDtypeStruct((2 * quarter, seg_len), f32),
                *band,
            ],
            in_specs=[VMEM] * 3,
            out_specs=[VMEM] * (3 + len(band)),
            compiler_params=PARAMS,
            cost_estimate=pl.CostEstimate(flops=10**8, bytes_accessed=8 * 2**20, transcendentals=0),
            name="columns",
        )(samples, following, flags)

    *near, band = column_side(0, jax.ShapeDtypeStruct((LANES // QB * (M + QB), LANES), bf16))
    total = pl.pallas_call(
        windows_kernel,
        out_shape=jax.ShapeDtypeStruct((quarter, turns * (M + 2 * QB)), f32),
        in_specs=[SMEM] * 2 + [ANY] + [VMEM] * GROUP,
        out_specs=VMEM,
        compiler_params=PARAMS,
        name="windows",
    )(owners, blocks, near[1], shares[0], arrived[1], arrived[2], arrived[3])

    rounds = rounds_beyond_group(devices_col)
    for masks in rounds[:-1]:
        total = sum([exchanged(total, mask) for mask in masks], total)
    order = (0, 2, 1) if len(rounds[-1]) == 3 else (0,)
    parts = [total] + [exchanged(total, rounds[-1][i]) for i in order]
    far = column_side(2)
    mine = pl.pallas_call(
        functools.partial(query_kernel, turns),
        out_shape=jax.ShapeDtypeStruct((quarter, turns * (M + 3 * QB)), f32),
        in_specs=[ANY] + [VMEM] * (1 + len(parts)),
        out_specs=VMEM,
        compiler_params=PARAMS,
        name="query_stats",
    )(far[1], band, *parts)
    others = {mask: exchanged(mine, mask) for mask in (3, 2, 1)}

    partial = jax.ShapeDtypeStruct((queries, seg_len), f32)
    summed = pl.pallas_call(
        functools.partial(first_kernel, turns),
        out_shape=partial,
        in_specs=[VMEM] * 5,
        out_specs=VMEM,
        compiler_params=PARAMS,
        cost_estimate=pl.CostEstimate(flops=5 * 10**8, bytes_accessed=4 * 2**20, transcendentals=0),
        name="first_two",
    )(mine, others[1], *near)
    summed = pl.pallas_call(
        functools.partial(next_kernel, turns),
        out_shape=partial,
        in_specs=[VMEM] * 5,
        out_specs=VMEM,
        compiler_params=PARAMS,
        cost_estimate=pl.CostEstimate(flops=2 * 10**8, bytes_accessed=2 * 2**20, transcendentals=0),
        name="third",
    )(others[2], *far, summed)
    rows, column = pl.pallas_call(
        functools.partial(last_kernel, turns, channels, limit),
        out_shape=[jax.ShapeDtypeStruct((turns, QB), f32), jax.ShapeDtypeStruct((1, seg_len), f32)],
        in_specs=[SMEM] * 3 + [VMEM] * 5,
        out_specs=[VMEM] * 2,
        compiler_params=PARAMS,
        name="fourth",
    )(owners, blocks, excl, others[3], *far, summed)

    small = [[masks[0] + 1, *(m + 1 for m in reversed(masks[1:]))] for masks in rounds]
    for masks in [[1, 2, 3], *small]:
        rows = functools.reduce(jnp.minimum, [exchanged(rows, mask) for mask in masks], rows)
    return (rows, column.reshape(seg_len))


def solution(mesh):
    return jax.shard_map(
        shards,
        mesh=mesh,
        in_specs=(P(None, ("grp", "col")), P(None, ("grp", "col")), P("grp"), P("grp"), P("grp")),
        out_specs=(P("grp", None), P(("grp", "col"))),
        check_vma=False,
    )
```

```python
import functools

import jax
import jax.numpy as jnp
from jax import lax
from jax.experimental import pallas as pl
from jax.experimental.pallas import tpu as pltpu
from jax.sharding import PartitionSpec as P

M = 256
QB = 32
CORES = 2
BASE = 4
LANES = 128

f32 = jnp.float32
bf16 = jnp.bfloat16


def exchanged(block, mask):
    devices = range(lax.axis_size("col"))
    return lax.ppermute(block, "col", [(i, i ^ mask) for i in devices])


def rounds_from(base, devices):
    rounds = []
    while base < devices:
        radix = 4 if (devices // base) % 4 == 0 else 2
        rounds.append([base * i for i in range(1, radix)])
        base *= radix
    return rounds


def split3(value):
    high = value.astype(bf16)
    rest = value - high.astype(f32)
    mid = rest.astype(bf16)
    low = (rest - mid.astype(f32)).astype(bf16)
    return high, mid, low


def half_rows(ref, which):
    half = ref.shape[0] // CORES
    return pl.ds(pl.multiple_of(which * half, half), half)


def share_kernel(packed, keep, send):
    core = lax.rem(lax.axis_index("col"), CORES)
    keep[...] = packed[half_rows(packed, core), :]
    send[...] = packed[half_rows(packed, 1 - core), :]


def chip_kernel(starts, own, other, out, both, starts_out):
    turns = starts.shape[0]
    half, width = own.shape[0], own.shape[1] // 2
    here = lax.axis_index("col")
    core = lax.rem(here, CORES)
    row = lax.broadcasted_iota(jnp.int32, (width, width), 0)
    col = lax.broadcasted_iota(jnp.int32, (width, width), 1)
    flip = (row + col == width - 1).astype(bf16)
    stack = jnp.concatenate(split3(own[:, :width]) + split3(other[:, :width]), axis=0)
    turned = jnp.dot(stack, flip, preferred_element_type=f32)
    for i in range(CORES):
        high, mid, low = (turned[(3 * i + j) * half : (3 * i + j + 1) * half] for j in range(3))
        out[:, i * width : (i + 1) * width] = low + mid + high
    for turn in range(turns):
        starts_out[turn : turn + 1, :] = jnp.full((1, LANES), starts[turn].astype(f32))
    both[core] = own[...]
    both[1 - core] = other[...]
    lane = lax.broadcasted_iota(jnp.int32, (half, LANES), 1)
    per_tile = LANES // QB
    for tile in range(turns // per_tile):
        valids = jnp.zeros((half, LANES), f32)
        for i in range(per_tile):
            start = starts[tile * per_tile + i]
            owner, shift = start // width, lax.rem(start, width)
            mine = (owner == here).astype(f32)
            others = (owner == here ^ 1).astype(f32)
            flags = mine * own[:, width:] + others * other[:, width:]
            flags = pltpu.roll(flags, lax.rem(width - shift, width), 1)[:, :LANES]
            if i:
                flags = pltpu.roll(flags, i * QB, 1)
            valids = jnp.where((lane >= i * QB) & (lane < (i + 1) * QB), flags, valids)
        at = 2 * width + tile * LANES
        out[:, at : at + LANES] = valids


def windows_kernel(masks, starts_ref, after, after_too, *refs):
    parts, out, lines = refs[: len(masks)], refs[len(masks)], refs[len(masks) + 1]
    turns = starts_ref.shape[0]
    starts = [jnp.max(starts_ref[turn : turn + 1, :]).astype(jnp.int32) for turn in range(turns)]
    half, width = out.shape[0], lines.shape[1]
    here = lax.axis_index("col")
    for i, part in enumerate(parts):
        for j in range(CORES):
            at = (CORES * i + j) * half
            lines[at : at + half, :] = part[:, j * width : (j + 1) * width]
    none = CORES * len(masks)
    lines[none * half :, :] = jnp.zeros((half, width), f32)
    held = sum(masks[i] for i in range(1, len(masks)) if masks[i] & (masks[i] - 1) == 0) + CORES - 1

    def segment(device):
        relative = device ^ here
        slot = CORES * ((relative & (held - CORES + 1)) // BASE) + (relative & (CORES - 1))
        slot = jnp.where((relative & held) == relative, slot, none)
        return lines[pl.ds(pl.multiple_of(slot * half, half), half), :]

    lane = lax.broadcasted_iota(jnp.int32, (half, width), 1)
    lane_128 = lax.broadcasted_iota(jnp.int32, (half, LANES), 1)
    per_tile = LANES // QB
    for tile in range(turns // per_tile):
        tails = jnp.zeros((half, LANES), f32)
        for i in range(per_tile):
            turn = tile * per_tile + i
            owner, split = starts[turn] // width, lax.rem(starts[turn], width) + QB
            amount = lax.rem(split, width)
            first = pltpu.roll(segment(owner), amount, 1)
            second = pltpu.roll(segment(owner + 1), amount, 1)
            out[:, turn * M : (turn + 1) * M] = jnp.where(lane >= split, first, second)
            tail = first[:, :LANES]
            if i:
                tail = pltpu.roll(tail, i * QB, 1)
            tails = jnp.where((lane_128 >= i * QB) & (lane_128 < (i + 1) * QB), tail, tails)
        at = turns * M + tile * LANES
        out[:, at : at + LANES] = tails
        at = turns * (M + QB) + tile * LANES
        flags = slice(2 * width + tile * LANES, 2 * width + (tile + 1) * LANES)
        out[:, at : at + LANES] = sum([part[:, flags] for part in parts[1:]], parts[0][:, flags])


def query_kernel(turns, after, band_ref, *refs):
    parts, out = refs[:-1], refs[-1]
    total = parts[0][...]
    for part in parts[1:]:
        total = total + part[...]
    samples = turns * (M + QB)
    per_tile = LANES // QB
    main, tail = [], []
    for tile in range(turns // per_tile):
        at = turns * M + tile * LANES
        tail_tile = total[:, at : at + LANES]
        lane = lax.broadcasted_iota(jnp.int32, tail_tile.shape, 1)
        centre = jnp.zeros_like(tail_tile)
        for i in range(per_tile):
            turn = tile * per_tile + i
            block = total[:, turn * M : (turn + 1) * M]
            mean = jnp.sum(block, axis=1, keepdims=True) * (1.0 / M)
            main.append(block - mean)
            centre = jnp.where((lane >= i * QB) & (lane < (i + 1) * QB), mean, centre)
        tail.append(tail_tile - centre)
    for tile in range(turns // per_tile):
        rows = main[tile * per_tile : (tile + 1) * per_tile] + [tail[tile]]
        shifted = jnp.concatenate(rows, axis=1)
        half = shifted.shape[0]
        stack = jnp.concatenate([*split3(shifted), *split3(shifted * shifted)], axis=0)
        sums = jnp.dot(stack, band_ref[...], preferred_element_type=f32)
        first = sums[2 * half : 3 * half] + sums[half : 2 * half] + sums[:half]
        second = sums[5 * half : 6 * half] + sums[4 * half : 5 * half] + sums[3 * half : 4 * half]
        mean = first * (1.0 / M)
        spread = second * (1.0 / M) - mean * mean
        at = samples + tile * LANES
        scale = total[:, at : at + LANES] / jnp.sqrt(spread + 1e-05)
        out[:, at : at + LANES] = scale
        out[:, at + turns * QB : at + turns * QB + LANES] = mean * scale
    for turn in range(turns):
        out[:, turn * M : (turn + 1) * M] = main[turn]
    for tile in range(turns // per_tile):
        at = turns * M + tile * LANES
        out[:, at : at + LANES] = tail[tile]


def band_matrix(shape):
    lane = lax.broadcasted_iota(jnp.int32, shape, 0)
    query = lax.broadcasted_iota(jnp.int32, shape, 1)
    per_tile = LANES // QB
    beyond = lane - per_tile * M
    turn = jnp.where(beyond < 0, lane // M, beyond // QB)
    place = jnp.where(beyond < 0, lane % M, M + beyond % QB)
    q = query % QB
    inside = (turn == query // QB) & (place >= QB - q) & (place <= M + QB - 1 - q)
    return jnp.where(inside, 1.0, 0.0).astype(bf16)


def segment_columns(own, following, hankel, scale_ref, offset_ref):
    width = scale_ref.shape[1]
    samples = own[:, :width]
    centre = jnp.sum(samples, axis=1, keepdims=True) * (1.0 / width)
    extended = jnp.concatenate([samples - centre, following[:, :width] - centre], axis=1)
    length = extended.shape[1]
    first, second = extended, extended * extended
    step = 1
    while step < M:
        first = first + pltpu.roll(first, length - step, 1)
        second = second + pltpu.roll(second, length - step, 1)
        step *= 2
    mean = first[:, :width] * (1.0 / M)
    spread = second[:, :width] * (1.0 / M) - mean * mean
    scale = own[:, width:] / jnp.sqrt(jnp.maximum(spread, 0.0) + 1e-05)
    scale_ref[...] = scale
    offset_ref[...] = mean * scale
    for c in range(extended.shape[0]):
        base = jnp.broadcast_to(extended[c : c + 1, :], (16, length))
        base = pltpu.roll(base, length - 15, 1, stride=1, stride_axis=0).astype(bf16)
        for b in range(M // 16):
            shift = M - 16 - 16 * b
            block = pltpu.roll(base, length - shift, 1) if shift else base
            hankel[c, 16 * b : 16 * (b + 1), :] = block[:, :width]


def first_columns_kernel(both, hankel, scale_ref, offset_ref, band_ref):
    band_ref[...] = band_matrix(band_ref.shape)
    segment_columns(both.at[0], both.at[1], hankel.at[0], scale_ref.at[0], offset_ref.at[0])


def second_columns_kernel(
    limit, starts, excl, both, following, hankel_in, scale_in, offset_in, hankel, scale_ref, offset_ref, banned, beyond
):
    width = banned.shape[1]
    columns = lax.axis_index("col") * width + lax.broadcasted_iota(jnp.int32, (QB, width), 1)
    apart = lax.broadcasted_iota(jnp.int32, (QB, width), 0) - columns
    last = jnp.where(columns > limit, 1.0, 0.0)
    for turn in range(starts.shape[0]):
        near = jnp.where(jnp.abs(apart + starts[turn]) < excl[0], 1.0, last)
        banned[turn * QB : (turn + 1) * QB, :] = near
    beyond[...] = last[:8]
    segment_columns(both.at[1], following, hankel.at[1], scale_ref.at[1], offset_ref.at[1])


def other_core_kernel(turns, y, hankel, scale_ref, offset_ref, out, windows_ref):
    queries = turns * QB
    samples = turns * (M + QB)
    per_tile = LANES // QB
    which = 1 - lax.rem(lax.axis_index("col"), CORES)
    by_query = jnp.transpose(y[:, samples : samples + queries])
    offsets = jnp.transpose(y[:, samples + queries : samples + 2 * queries])
    lines = []
    for turn in range(turns):
        at = turns * M + (turn // per_tile) * LANES
        tail = y[:, at : at + LANES]
        if turn % per_tile:
            tail = pltpu.roll(tail, LANES - (turn % per_tile) * QB, 1)
        lines.append(jnp.concatenate([y[:, turn * M : (turn + 1) * M], tail], axis=1))
    length = M + LANES
    acc = -M * jnp.dot(offsets, offset_ref[which], preferred_element_type=f32, precision=lax.Precision.HIGHEST)
    for c in range(y.shape[0]):
        scale = by_query[:, c : c + 1]
        windows = []
        for turn in range(turns):
            row = jnp.broadcast_to(lines[turn][c : c + 1, :], (QB, length))
            row = pltpu.roll(row, length - QB, 1, stride=1, stride_axis=0)
            windows.append((row[:, :M] * scale[turn * QB : (turn + 1) * QB]).astype(bf16))
        windows = jnp.concatenate(windows, axis=0)
        windows_ref[c] = windows
        products = jnp.dot(windows, hankel[which, c], preferred_element_type=f32)
        acc = acc + products * scale_ref[which, c : c + 1, :]
    out[...] = acc


def own_core_kernel(turns, y, windows_ref, hankel, scale_ref, offset_ref, out):
    queries = turns * QB
    at = turns * (M + QB) + queries
    which = lax.rem(lax.axis_index("col"), CORES)
    offsets = jnp.transpose(y[:, at : at + queries])
    acc = -M * jnp.dot(offsets, offset_ref[which], preferred_element_type=f32, precision=lax.Precision.HIGHEST)
    for c in range(y.shape[0]):
        products = jnp.dot(windows_ref[c], hankel[which, c], preferred_element_type=f32)
        acc = acc + products * scale_ref[which, c : c + 1, :]
    out[...] = acc


def minima_kernel(turns, channels, own, other, banned, beyond, row_out, col_out):
    distance = 1.0 - (own[...] + other[...]) * (1.0 / (M * channels))
    distance = jnp.where(banned[...] > 0.0, 4.0, distance)
    width = distance.shape[1]
    column_min = jnp.min(distance, axis=0, keepdims=True)
    col_out[...] = jnp.where(beyond[:1, :] > 0.0, 0.0, column_min)
    narrow = distance[:, :LANES]
    for at in range(LANES, width, LANES):
        narrow = jnp.minimum(narrow, distance[:, at : at + LANES])
    flat = jnp.min(jnp.transpose(narrow), axis=0, keepdims=True)
    for turn in range(turns):
        row_out[turn : turn + 1, :] = flat[:, turn * QB : (turn + 1) * QB]


SPECS = dict(
    v=pl.BlockSpec(memory_space=pltpu.VMEM), s=pl.BlockSpec(memory_space=pltpu.SMEM), a=pl.BlockSpec(memory_space=pl.ANY)
)


def call(kernel, name, out_shape, spaces, *operands, flops=10**6, **options):
    many = isinstance(out_shape, list)
    return pl.pallas_call(
        kernel,
        out_shape=out_shape,
        in_specs=[SPECS[space] for space in spaces],
        out_specs=[SPECS["v"]] * len(out_shape) if many else SPECS["v"],
        compiler_params=pltpu.CompilerParams(vmem_limit_bytes=40 * 2**20),
        cost_estimate=pl.CostEstimate(flops=flops, bytes_accessed=2**20, transcendentals=0),
        name=name,
        **options,
    )(*operands)


def shards(series, valid, owners, blocks, excl):
    channels, seg_len = series.shape
    devices_col = lax.axis_size("col")
    turns = owners.shape[0]
    half = channels // CORES
    queries = turns * QB
    limit = seg_len * devices_col - M
    starts = owners * seg_len + blocks * QB

    packed = jnp.concatenate([series, valid.astype(f32)], axis=1)
    part = jax.ShapeDtypeStruct((half, 2 * seg_len), f32)
    keep, send = call(share_kernel, "share", [part] * 2, "v", packed)
    chip, both, starts_vector = call(
        chip_kernel,
        "chip",
        [
            jax.ShapeDtypeStruct((half, 2 * seg_len + queries), f32),
            jax.ShapeDtypeStruct((CORES, half, 2 * seg_len), f32),
            jax.ShapeDtypeStruct((turns, LANES), f32),
        ],
        "svv",
        starts,
        keep,
        exchanged(send, 1),
    )
    back = [(i, (i - CORES) % devices_col) for i in range(devices_col)]
    following = lax.ppermute(both[0, :, :seg_len], "col", back)

    side = [
        jax.ShapeDtypeStruct((CORES, half, M, seg_len), bf16),
        jax.ShapeDtypeStruct((CORES, half, seg_len), f32),
        jax.ShapeDtypeStruct((CORES, half, seg_len), f32),
    ]
    band = jax.ShapeDtypeStruct((LANES // QB * (M + QB), LANES), bf16)
    *columns, band = call(first_columns_kernel, "columns", [*side, band], "v", both, flops=10**8)

    rounds = rounds_from(BASE, devices_col)
    masks = [0, *rounds[0]]
    total = call(
        functools.partial(windows_kernel, masks),
        "windows",
        jax.ShapeDtypeStruct((half, turns * (M + 2 * QB)), f32),
        "vaa" + "v" * len(masks),
        starts_vector,
        columns[1],
        following,
        chip,
        *[exchanged(chip, mask) for mask in rounds[0]],
        scratch_shapes=[pltpu.VMEM(((CORES * len(masks) + 1) * half, seg_len), f32)],
    )
    for others in rounds[1:]:
        total = sum([exchanged(total, mask) for mask in others], total)
    *columns, banned, beyond = call(
        functools.partial(second_columns_kernel, limit),
        "columns",
        [*side, jax.ShapeDtypeStruct((queries, seg_len), f32), jax.ShapeDtypeStruct((8, seg_len), f32)],
        "ssvvaaa",
        starts,
        excl,
        both,
        following,
        *columns,
        input_output_aliases={4: 0, 5: 1, 6: 2},
        flops=10**8,
    )
    queried = call(
        functools.partial(query_kernel, turns),
        "query_stats",
        jax.ShapeDtypeStruct((half, turns * (M + 3 * QB)), f32),
        "avvv",
        columns[1],
        band,
        total,
        exchanged(total, CORES),
    )
    partial = jax.ShapeDtypeStruct((queries, seg_len), f32)
    theirs, windows = call(
        functools.partial(other_core_kernel, turns),
        "other_core",
        [partial, jax.ShapeDtypeStruct((half, queries, M), bf16)],
        "vvvv",
        queried,
        *columns,
    )
    mine = call(
        functools.partial(own_core_kernel, turns),
        "own_core",
        partial,
        "vvvvv",
        queried,
        windows,
        *columns,
        flops=5 * 10**8,
    )
    rows, column = call(
        functools.partial(minima_kernel, turns, channels),
        "minima",
        [jax.ShapeDtypeStruct((turns, QB), f32), jax.ShapeDtypeStruct((1, seg_len), f32)],
        "vvvv",
        mine,
        exchanged(theirs, 1),
        banned,
        beyond,
    )
    crossed = [[others[0] + 1, *(mask + 1 for mask in reversed(others[1:]))] for others in rounds]
    for others in [[1, 2, 3], *crossed]:
        rows = functools.reduce(jnp.minimum, [exchanged(rows, mask) for mask in others], rows)
    return (rows, column.reshape(seg_len))


def solution(mesh):
    return jax.shard_map(
        shards,
        mesh=mesh,
        in_specs=(P(None, ("grp", "col")), P(None, ("grp", "col")), P("grp"), P("grp"), P("grp")),
        out_specs=(P("grp", None), P(("grp", "col"))),
        check_vma=False,
    )
```

```python
import functools

import jax
import jax.numpy as jnp
from jax import lax
from jax.experimental import pallas as pl
from jax.experimental.pallas import tpu as pltpu
from jax.sharding import PartitionSpec as P

M = 256
QB = 32
CORES = 2
BASE = 4
LANES = 128

f32 = jnp.float32
bf16 = jnp.bfloat16


def exchanged(block, mask):
    devices = range(lax.axis_size("col"))
    return lax.ppermute(block, "col", [(i, i ^ mask) for i in devices])


def rounds_from(base, devices):
    rounds = []
    while base < devices:
        radix = 4 if (devices // base) % 4 == 0 else 2
        rounds.append([base * i for i in range(1, radix)])
        base *= radix
    return rounds


def split3(value):
    high = value.astype(bf16)
    rest = value - high.astype(f32)
    mid = rest.astype(bf16)
    low = (rest - mid.astype(f32)).astype(bf16)
    return high, mid, low


def half_rows(ref, which):
    half = ref.shape[0]
    return pl.ds(pl.multiple_of(which * half, half), half)


def share_kernel(packed, keep, send):
    core = lax.rem(lax.axis_index("col"), CORES)
    width = packed.shape[2]
    for which, out in ((core, keep), (1 - core, send)):
        for i in range(packed.shape[0]):
            out[:, i * width : (i + 1) * width] = packed[i, half_rows(out, which), :]


def first_lane(ref):
    return [jnp.max(ref[row : row + 1, :]).astype(jnp.int32) for row in range(ref.shape[0])]


def chip_kernel(starts_ref, own, other, out, both):
    turns = starts_ref.shape[0]
    starts = first_lane(starts_ref)
    half, width = own.shape[0], own.shape[1] // 2
    here = lax.axis_index("col")
    core = lax.rem(here, CORES)
    row = lax.broadcasted_iota(jnp.int32, (width, width), 0)
    col = lax.broadcasted_iota(jnp.int32, (width, width), 1)
    flip = (row + col == width - 1).astype(bf16)
    stack = jnp.concatenate(split3(own[:, :width]) + split3(other[:, :width]), axis=0)
    turned = jnp.dot(stack, flip, preferred_element_type=f32)
    for i in range(CORES):
        high, mid, low = (turned[(3 * i + j) * half : (3 * i + j + 1) * half] for j in range(3))
        out[:, i * width : (i + 1) * width] = low + mid + high
    both[core] = own[...]
    both[1 - core] = other[...]
    lane = lax.broadcasted_iota(jnp.int32, (half, LANES), 1)
    per_tile = LANES // QB
    for tile in range(turns // per_tile):
        valids = jnp.zeros((half, LANES), f32)
        for i in range(per_tile):
            start = starts[tile * per_tile + i]
            owner, shift = start // width, lax.rem(start, width)
            mine = (owner == here).astype(f32)
            others = (owner == here ^ 1).astype(f32)
            flags = mine * own[:, width:] + others * other[:, width:]
            flags = pltpu.roll(flags, lax.rem(width - shift, width), 1)[:, :LANES]
            if i:
                flags = pltpu.roll(flags, i * QB, 1)
            valids = jnp.where((lane >= i * QB) & (lane < (i + 1) * QB), flags, valids)
        at = 2 * width + tile * LANES
        out[:, at : at + LANES] = valids


def windows_kernel(masks, starts_ref, after, after_too, *refs):
    parts, out, lines = refs[: len(masks)], refs[len(masks)], refs[len(masks) + 1]
    turns = starts_ref.shape[0]
    starts = first_lane(starts_ref)
    half, width = out.shape[0], lines.shape[1]
    here = lax.axis_index("col")
    for i, part in enumerate(parts):
        for j in range(CORES):
            at = (CORES * i + j) * half
            lines[at : at + half, :] = part[:, j * width : (j + 1) * width]
    none = CORES * len(masks)
    lines[none * half :, :] = jnp.zeros((half, width), f32)
    held = sum(masks[i] for i in range(1, len(masks)) if masks[i] & (masks[i] - 1) == 0) + CORES - 1

    def segment(device):
        relative = device ^ here
        slot = CORES * ((relative & (held - CORES + 1)) // BASE) + (relative & (CORES - 1))
        slot = jnp.where((relative & held) == relative, slot, none)
        return lines[pl.ds(pl.multiple_of(slot * half, half), half), :]

    lane = lax.broadcasted_iota(jnp.int32, (half, width), 1)
    lane_128 = lax.broadcasted_iota(jnp.int32, (half, LANES), 1)
    per_tile = LANES // QB
    for tile in range(turns // per_tile):
        tails = jnp.zeros((half, LANES), f32)
        for i in range(per_tile):
            turn = tile * per_tile + i
            owner, split = starts[turn] // width, lax.rem(starts[turn], width) + QB
            amount = lax.rem(split, width)
            first = pltpu.roll(segment(owner), amount, 1)
            second = pltpu.roll(segment(owner + 1), amount, 1)
            out[:, turn * M : (turn + 1) * M] = jnp.where(lane >= split, first, second)
            tail = first[:, :LANES]
            if i:
                tail = pltpu.roll(tail, i * QB, 1)
            tails = jnp.where((lane_128 >= i * QB) & (lane_128 < (i + 1) * QB), tail, tails)
        at = turns * M + tile * LANES
        out[:, at : at + LANES] = tails
        at = turns * (M + QB) + tile * LANES
        flags = slice(2 * width + tile * LANES, 2 * width + (tile + 1) * LANES)
        out[:, at : at + LANES] = sum([part[:, flags] for part in parts[1:]], parts[0][:, flags])


def query_kernel(turns, after, band_ref, *refs):
    parts, out = refs[:-1], refs[-1]
    total = parts[0][...]
    for part in parts[1:]:
        total = total + part[...]
    samples = turns * (M + QB)
    per_tile = LANES // QB
    main, tail = [], []
    for tile in range(turns // per_tile):
        at = turns * M + tile * LANES
        tail_tile = total[:, at : at + LANES]
        lane = lax.broadcasted_iota(jnp.int32, tail_tile.shape, 1)
        centre = jnp.zeros_like(tail_tile)
        for i in range(per_tile):
            turn = tile * per_tile + i
            block = total[:, turn * M : (turn + 1) * M]
            mean = jnp.sum(block, axis=1, keepdims=True) * (1.0 / M)
            main.append(block - mean)
            centre = jnp.where((lane >= i * QB) & (lane < (i + 1) * QB), mean, centre)
        tail.append(tail_tile - centre)
    for tile in range(turns // per_tile):
        rows = main[tile * per_tile : (tile + 1) * per_tile] + [tail[tile]]
        shifted = jnp.concatenate(rows, axis=1)
        half = shifted.shape[0]
        stack = jnp.concatenate([*split3(shifted), *split3(shifted * shifted)], axis=0)
        sums = jnp.dot(stack, band_ref[...], preferred_element_type=f32)
        first = sums[2 * half : 3 * half] + sums[half : 2 * half] + sums[:half]
        second = sums[5 * half : 6 * half] + sums[4 * half : 5 * half] + sums[3 * half : 4 * half]
        mean = first * (1.0 / M)
        spread = second * (1.0 / M) - mean * mean
        at = samples + tile * LANES
        scale = total[:, at : at + LANES] / jnp.sqrt(spread + 1e-05)
        out[:, at : at + LANES] = scale
        out[:, at + turns * QB : at + turns * QB + LANES] = mean * scale
    for turn in range(turns):
        out[:, turn * M : (turn + 1) * M] = main[turn]
    for tile in range(turns // per_tile):
        at = turns * M + tile * LANES
        out[:, at : at + LANES] = tail[tile]


def band_matrix(shape):
    lane = lax.broadcasted_iota(jnp.int32, shape, 0)
    query = lax.broadcasted_iota(jnp.int32, shape, 1)
    per_tile = LANES // QB
    beyond = lane - per_tile * M
    turn = jnp.where(beyond < 0, lane // M, beyond // QB)
    place = jnp.where(beyond < 0, lane % M, M + beyond % QB)
    q = query % QB
    inside = (turn == query // QB) & (place >= QB - q) & (place <= M + QB - 1 - q)
    return jnp.where(inside, 1.0, 0.0).astype(bf16)


def column_band(shape):
    row = lax.broadcasted_iota(jnp.int32, shape, 0)
    col = lax.broadcasted_iota(jnp.int32, shape, 1)
    return jnp.where((row >= col) & (row < col + M), 1.0, 0.0).astype(bf16)


def segment_columns(own, following, band, hankel, scale_ref, offset_ref):
    width = scale_ref.shape[1]
    samples = own[:, :width]
    centre = jnp.sum(samples, axis=1, keepdims=True) * (1.0 / width)
    extended = jnp.concatenate([samples - centre, following[:, :width] - centre], axis=1)
    length = extended.shape[1]
    channels = extended.shape[0]
    stack = jnp.concatenate([*split3(extended), *split3(extended * extended)], axis=0)
    sums = jnp.dot(stack, band[...], preferred_element_type=f32)
    first, first_mid, first_low, second, second_mid, second_low = (
        sums[i * channels : (i + 1) * channels] for i in range(6)
    )
    mean = (first_low + first_mid + first) * (1.0 / M)
    spread = (second_low + second_mid + second) * (1.0 / M) - mean * mean
    scale = own[:, width:] / jnp.sqrt(jnp.maximum(spread, 0.0) + 1e-05)
    scale_ref[...] = scale
    offset_ref[...] = mean * scale
    for c in range(channels):
        base = jnp.broadcast_to(extended[c : c + 1, :], (LANES, length))
        base = pltpu.roll(base, length - LANES + 1, 1, stride=1, stride_axis=0).astype(bf16)
        for high in range(M // LANES):
            at = M - LANES - high * LANES
            hankel[c, at : at + LANES, :] = base[:, high * LANES : high * LANES + width]


def first_columns_kernel(both, hankel, scale_ref, offset_ref, band_ref, sums_ref, spread_ref):
    spread_ref[...] = spread_matrix(spread_ref.shape)
    band_ref[...] = band_matrix(band_ref.shape)
    sums_ref[...] = column_band(sums_ref.shape)
    segment_columns(both.at[0], both.at[1], sums_ref, hankel.at[0], scale_ref.at[0], offset_ref.at[0])


def second_columns_kernel(
    limit, starts, excl, both, following, sums_ref, hankel_in, scale_in, offset_in, hankel, scale_ref, offset_ref, banned, beyond
):
    width = banned.shape[1]
    columns = lax.axis_index("col") * width + lax.broadcasted_iota(jnp.int32, (QB, width), 1)
    apart = lax.broadcasted_iota(jnp.int32, (QB, width), 0) - columns
    last = jnp.where(columns > limit, 1.0, 0.0)
    for turn in range(starts.shape[0]):
        near = jnp.where(jnp.abs(apart + starts[turn]) < excl[0], 1.0, last)
        banned[turn * QB : (turn + 1) * QB, :] = near
    beyond[...] = last[:8]
    segment_columns(both.at[1], following, sums_ref, hankel.at[1], scale_ref.at[1], offset_ref.at[1])


def spread_matrix(shape):
    row = lax.broadcasted_iota(jnp.int32, shape, 0)
    tile = lax.broadcasted_iota(jnp.int32, shape, 1) // LANES
    channels = shape[0] // 2
    return jnp.where((row == tile) | (row == tile + channels), 1.0, 0.0).astype(bf16)


def covariances(offsets, windows_ref, hankel, scale_ref, offset_ref, which):
    acc = -M * jnp.dot(offsets, offset_ref[which], preferred_element_type=f32, precision=lax.Precision.HIGHEST)
    for c in range(windows_ref.shape[0]):
        products = jnp.dot(windows_ref[c], hankel[which, c], preferred_element_type=f32)
        acc = acc + products * scale_ref[which, c : c + 1, :]
    return acc


def other_core_kernel(turns, y, spread_ref, hankel, scale_ref, offset_ref, out, windows_ref, scales):
    queries = turns * QB
    samples = turns * (M + QB)
    per_tile = LANES // QB
    by_query = jnp.transpose(y[:, samples : samples + queries])
    offsets = jnp.transpose(y[:, samples + queries : samples + 2 * queries])
    high = by_query.astype(bf16)
    low = (by_query - high.astype(f32)).astype(bf16)
    scales[...] = jnp.dot(jnp.concatenate([high, low], axis=1), spread_ref[...], preferred_element_type=f32)
    lines = []
    for turn in range(turns):
        at = turns * M + (turn // per_tile) * LANES
        tail = y[:, at : at + LANES]
        if turn % per_tile:
            tail = pltpu.roll(tail, LANES - (turn % per_tile) * QB, 1)
        lines.append(jnp.concatenate([y[:, turn * M : (turn + 1) * M], tail], axis=1))
    which = 1 - lax.rem(lax.axis_index("col"), CORES)
    acc = -M * jnp.dot(offsets, offset_ref[which], preferred_element_type=f32, precision=lax.Precision.HIGHEST)
    for c in range(y.shape[0]):
        windows = []
        for turn in range(turns):
            row = jnp.broadcast_to(lines[turn][c : c + 1, :], (QB, M + LANES))
            row = pltpu.roll(row, M + LANES - QB, 1, stride=1, stride_axis=0)
            scale = scales[turn * QB : (turn + 1) * QB, c * LANES : (c + 1) * LANES]
            scaled = [row[:, k : k + LANES] * scale for k in range(0, M, LANES)]
            windows.append(jnp.concatenate(scaled, axis=1).astype(bf16))
        windows = jnp.concatenate(windows, axis=0)
        windows_ref[c] = windows
        products = jnp.dot(windows, hankel[which, c], preferred_element_type=f32)
        acc = acc + products * scale_ref[which, c : c + 1, :]
    out[...] = acc


def own_core_kernel(turns, y, windows_ref, hankel, scale_ref, offset_ref, out):
    queries = turns * QB
    at = turns * (M + QB) + queries
    offsets = jnp.transpose(y[:, at : at + queries])
    which = lax.rem(lax.axis_index("col"), CORES)
    out[...] = covariances(offsets, windows_ref, hankel, scale_ref, offset_ref, which)


def minima_kernel(turns, channels, own, other, banned, beyond, row_out, col_out):
    distance = 1.0 - (own[...] + other[...]) * (1.0 / (M * channels))
    distance = jnp.where(banned[...] > 0.0, 4.0, distance)
    width = distance.shape[1]
    column_min = jnp.min(distance, axis=0, keepdims=True)
    col_out[...] = jnp.where(beyond[:1, :] > 0.0, 0.0, column_min)
    narrow = distance[:, :LANES]
    for at in range(LANES, width, LANES):
        narrow = jnp.minimum(narrow, distance[:, at : at + LANES])
    flat = jnp.min(jnp.transpose(narrow), axis=0, keepdims=True)
    for turn in range(turns):
        row_out[turn : turn + 1, :] = flat[:, turn * QB : (turn + 1) * QB]


SPECS = dict(
    v=pl.BlockSpec(memory_space=pltpu.VMEM), s=pl.BlockSpec(memory_space=pltpu.SMEM), a=pl.BlockSpec(memory_space=pl.ANY)
)


def call(kernel, name, out_shape, spaces, *operands, flops=10**6, **options):
    many = isinstance(out_shape, list)
    return pl.pallas_call(
        kernel,
        out_shape=out_shape,
        in_specs=[SPECS[space] for space in spaces],
        out_specs=[SPECS["v"]] * len(out_shape) if many else SPECS["v"],
        compiler_params=pltpu.CompilerParams(vmem_limit_bytes=40 * 2**20),
        cost_estimate=pl.CostEstimate(flops=flops, bytes_accessed=2**20, transcendentals=0),
        name=name,
        **options,
    )(*operands)


def shards(series, valid, owners, blocks, excl):
    channels, seg_len = series.shape
    devices_col = lax.axis_size("col")
    turns = owners.shape[0]
    half = channels // CORES
    queries = turns * QB
    limit = seg_len * devices_col - M
    starts = owners * seg_len + blocks * QB
    starts_vector = jnp.broadcast_to(starts.astype(f32)[:, None], (turns, LANES))

    which = lax.broadcasted_iota(jnp.int32, (2, *series.shape), 0)
    packed = jnp.where(which == 0, series[None], valid[None].astype(f32))
    part = jax.ShapeDtypeStruct((half, 2 * seg_len), f32)
    keep, send = call(share_kernel, "share", [part] * 2, "v", packed)
    chip, both = call(
        chip_kernel,
        "chip",
        [
            jax.ShapeDtypeStruct((half, 2 * seg_len + queries), f32),
            jax.ShapeDtypeStruct((CORES, half, 2 * seg_len), f32),
        ],
        "vvv",
        starts_vector,
        keep,
        exchanged(send, 1),
    )
    back = [(i, (i - CORES) % devices_col) for i in range(devices_col)]
    following = lax.ppermute(both[0, :, :seg_len], "col", back)

    side = [
        jax.ShapeDtypeStruct((CORES, half, M, seg_len), bf16),
        jax.ShapeDtypeStruct((CORES, half, seg_len), f32),
        jax.ShapeDtypeStruct((CORES, half, seg_len), f32),
    ]
    band = jax.ShapeDtypeStruct((LANES // QB * (M + QB), LANES), bf16)
    sums = jax.ShapeDtypeStruct((2 * seg_len, seg_len), bf16)
    spread = jax.ShapeDtypeStruct((2 * half, half * LANES), bf16)
    *columns, band, sums, spread = call(
        first_columns_kernel, "columns", [*side, band, sums, spread], "v", both, flops=10**8
    )

    rounds = rounds_from(BASE, devices_col)
    masks = [0, *rounds[0]]
    total = call(
        functools.partial(windows_kernel, masks),
        "windows",
        jax.ShapeDtypeStruct((half, turns * (M + 2 * QB)), f32),
        "vaa" + "v" * len(masks),
        starts_vector,
        columns[1],
        following,
        chip,
        *[exchanged(chip, mask) for mask in rounds[0]],
        scratch_shapes=[pltpu.VMEM(((CORES * len(masks) + 1) * half, seg_len), f32)],
    )
    for others in rounds[1:]:
        total = sum([exchanged(total, mask) for mask in others], total)
    *columns, banned, beyond = call(
        functools.partial(second_columns_kernel, limit),
        "columns",
        [*side, jax.ShapeDtypeStruct((queries, seg_len), f32), jax.ShapeDtypeStruct((8, seg_len), f32)],
        "ssvvvaaa",
        starts,
        excl,
        both,
        following,
        sums,
        *columns,
        input_output_aliases={5: 0, 6: 1, 7: 2},
        flops=10**8,
    )
    queried = call(
        functools.partial(query_kernel, turns),
        "query_stats",
        jax.ShapeDtypeStruct((half, turns * (M + 3 * QB)), f32),
        "avvv",
        columns[1],
        band,
        total,
        exchanged(total, CORES),
    )
    partial = jax.ShapeDtypeStruct((queries, seg_len), f32)
    theirs, windows = call(
        functools.partial(other_core_kernel, turns),
        "other_core",
        [partial, jax.ShapeDtypeStruct((half, queries, M), bf16)],
        "vvvvv",
        queried,
        spread,
        *columns,
        scratch_shapes=[pltpu.VMEM((queries, half * LANES), f32)],
    )
    mine = call(
        functools.partial(own_core_kernel, turns),
        "own_core",
        partial,
        "vvvvv",
        queried,
        windows,
        *columns,
        flops=5 * 10**8,
    )
    rows, column = call(
        functools.partial(minima_kernel, turns, channels),
        "minima",
        [jax.ShapeDtypeStruct((turns, QB), f32), jax.ShapeDtypeStruct((1, seg_len), f32)],
        "vvvv",
        mine,
        exchanged(theirs, 1),
        banned,
        beyond,
    )
    crossed = [[others[0] + 1, *(mask + 1 for mask in reversed(others[1:]))] for others in rounds]
    for others in [[1, 2, 3], *crossed]:
        rows = functools.reduce(jnp.minimum, [exchanged(rows, mask) for mask in others], rows)
    return (rows, column.reshape(seg_len))


def solution(mesh):
    return jax.shard_map(
        shards,
        mesh=mesh,
        in_specs=(P(None, ("grp", "col")), P(None, ("grp", "col")), P("grp"), P("grp"), P("grp")),
        out_specs=(P("grp", None), P(("grp", "col"))),
        check_vma=False,
    )
```

```python
import functools

import jax
import jax.numpy as jnp
from jax import lax
from jax.experimental import pallas as pl
from jax.experimental.pallas import tpu as pltpu
from jax.sharding import PartitionSpec as P

M = 256
QB = 32
CORES = 2
BASE = 4
LANES = 128

f32 = jnp.float32
bf16 = jnp.bfloat16


def exchanged(block, mask):
    devices = range(lax.axis_size("col"))
    return lax.ppermute(block, "col", [(i, i ^ mask) for i in devices])


def rounds_from(base, devices):
    rounds = []
    while base < devices:
        radix = 4 if (devices // base) % 4 == 0 else 2
        rounds.append([base * i for i in range(1, radix)])
        base *= radix
    return rounds


def split3(value):
    high = value.astype(bf16)
    rest = value - high.astype(f32)
    mid = rest.astype(bf16)
    low = (rest - mid.astype(f32)).astype(bf16)
    return high, mid, low


def half_rows(ref, which):
    half = ref.shape[0]
    return pl.ds(pl.multiple_of(which * half, half), half)


def share_kernel(packed, keep, send):
    core = lax.rem(lax.axis_index("col"), CORES)
    width = packed.shape[2]
    for which, out in ((core, keep), (1 - core, send)):
        for i in range(packed.shape[0]):
            out[:, i * width : (i + 1) * width] = packed[i, half_rows(out, which), :]


def first_lane(ref):
    return [jnp.max(ref[row : row + 1, :]).astype(jnp.int32) for row in range(ref.shape[0])]


def chip_kernel(starts_ref, own, other, out, both):
    turns = starts_ref.shape[0]
    starts = first_lane(starts_ref)
    half, width = own.shape[0], own.shape[1] // 2
    here = lax.axis_index("col")
    core = lax.rem(here, CORES)
    row = lax.broadcasted_iota(jnp.int32, (width, width), 0)
    col = lax.broadcasted_iota(jnp.int32, (width, width), 1)
    flip = (row + col == width - 1).astype(bf16)
    stack = jnp.concatenate(split3(own[:, :width]) + split3(other[:, :width]), axis=0)
    turned = jnp.dot(stack, flip, preferred_element_type=f32)
    for i in range(CORES):
        high, mid, low = (turned[(3 * i + j) * half : (3 * i + j + 1) * half] for j in range(3))
        out[:, i * width : (i + 1) * width] = low + mid + high
    both[core] = own[...]
    both[1 - core] = other[...]
    lane = lax.broadcasted_iota(jnp.int32, (half, LANES), 1)
    per_tile = LANES // QB
    for tile in range(turns // per_tile):
        valids = jnp.zeros((half, LANES), f32)
        for i in range(per_tile):
            start = starts[tile * per_tile + i]
            owner, shift = start // width, lax.rem(start, width)
            mine = (owner == here).astype(f32)
            others = (owner == here ^ 1).astype(f32)
            flags = mine * own[:, width:] + others * other[:, width:]
            flags = pltpu.roll(flags, lax.rem(width - shift, width), 1)[:, :LANES]
            if i:
                flags = pltpu.roll(flags, i * QB, 1)
            valids = jnp.where((lane >= i * QB) & (lane < (i + 1) * QB), flags, valids)
        at = 2 * width + tile * LANES
        out[:, at : at + LANES] = valids


def windows_kernel(masks, starts_ref, after, after_too, *refs):
    parts, out, lines = refs[: len(masks)], refs[len(masks)], refs[len(masks) + 1]
    turns = starts_ref.shape[0]
    starts = first_lane(starts_ref)
    half, width = out.shape[0], lines.shape[1]
    here = lax.axis_index("col")
    for i, part in enumerate(parts):
        for j in range(CORES):
            at = (CORES * i + j) * half
            lines[at : at + half, :] = part[:, j * width : (j + 1) * width]
    none = CORES * len(masks)
    lines[none * half :, :] = jnp.zeros((half, width), f32)
    held = sum(masks[i] for i in range(1, len(masks)) if masks[i] & (masks[i] - 1) == 0) + CORES - 1

    def segment(device):
        relative = device ^ here
        slot = CORES * ((relative & (held - CORES + 1)) // BASE) + (relative & (CORES - 1))
        slot = jnp.where((relative & held) == relative, slot, none)
        return lines[pl.ds(pl.multiple_of(slot * half, half), half), :]

    lane = lax.broadcasted_iota(jnp.int32, (half, width), 1)
    lane_128 = lax.broadcasted_iota(jnp.int32, (half, LANES), 1)
    per_tile = LANES // QB
    for tile in range(turns // per_tile):
        tails = jnp.zeros((half, LANES), f32)
        for i in range(per_tile):
            turn = tile * per_tile + i
            owner, split = starts[turn] // width, lax.rem(starts[turn], width) + QB
            amount = lax.rem(split, width)
            first = pltpu.roll(segment(owner), amount, 1)
            second = pltpu.roll(segment(owner + 1), amount, 1)
            out[:, turn * M : (turn + 1) * M] = jnp.where(lane >= split, first, second)
            tail = first[:, :LANES]
            if i:
                tail = pltpu.roll(tail, i * QB, 1)
            tails = jnp.where((lane_128 >= i * QB) & (lane_128 < (i + 1) * QB), tail, tails)
        at = turns * M + tile * LANES
        out[:, at : at + LANES] = tails
        at = turns * (M + QB) + tile * LANES
        flags = slice(2 * width + tile * LANES, 2 * width + (tile + 1) * LANES)
        out[:, at : at + LANES] = sum([part[:, flags] for part in parts[1:]], parts[0][:, flags])


def query_kernel(turns, after, band_ref, *refs):
    parts, out = refs[:-1], refs[-1]
    total = parts[0][...]
    for part in parts[1:]:
        total = total + part[...]
    samples = turns * (M + QB)
    per_tile = LANES // QB
    main, tail = [], []
    for tile in range(turns // per_tile):
        at = turns * M + tile * LANES
        tail_tile = total[:, at : at + LANES]
        lane = lax.broadcasted_iota(jnp.int32, tail_tile.shape, 1)
        centre = jnp.zeros_like(tail_tile)
        for i in range(per_tile):
            turn = tile * per_tile + i
            block = total[:, turn * M : (turn + 1) * M]
            mean = jnp.sum(block, axis=1, keepdims=True) * (1.0 / M)
            main.append(block - mean)
            centre = jnp.where((lane >= i * QB) & (lane < (i + 1) * QB), mean, centre)
        tail.append(tail_tile - centre)
    for tile in range(turns // per_tile):
        rows = main[tile * per_tile : (tile + 1) * per_tile] + [tail[tile]]
        shifted = jnp.concatenate(rows, axis=1)
        half = shifted.shape[0]
        stack = jnp.concatenate([*split3(shifted), *split3(shifted * shifted)], axis=0)
        sums = jnp.dot(stack, band_ref[...], preferred_element_type=f32)
        first = sums[2 * half : 3 * half] + sums[half : 2 * half] + sums[:half]
        second = sums[5 * half : 6 * half] + sums[4 * half : 5 * half] + sums[3 * half : 4 * half]
        mean = first * (1.0 / M)
        spread = second * (1.0 / M) - mean * mean
        at = samples + tile * LANES
        scale = total[:, at : at + LANES] / jnp.sqrt(spread + 1e-05)
        out[:, at : at + LANES] = scale
        out[:, at + turns * QB : at + turns * QB + LANES] = mean * scale
    for turn in range(turns):
        out[:, turn * M : (turn + 1) * M] = main[turn]
    for tile in range(turns // per_tile):
        at = turns * M + tile * LANES
        out[:, at : at + LANES] = tail[tile]


def band_matrix(shape):
    lane = lax.broadcasted_iota(jnp.int32, shape, 0)
    query = lax.broadcasted_iota(jnp.int32, shape, 1)
    per_tile = LANES // QB
    beyond = lane - per_tile * M
    turn = jnp.where(beyond < 0, lane // M, beyond // QB)
    place = jnp.where(beyond < 0, lane % M, M + beyond % QB)
    q = query % QB
    inside = (turn == query // QB) & (place >= QB - q) & (place <= M + QB - 1 - q)
    return jnp.where(inside, 1.0, 0.0).astype(bf16)


def column_band(shape):
    row = lax.broadcasted_iota(jnp.int32, shape, 0)
    col = lax.broadcasted_iota(jnp.int32, shape, 1)
    return jnp.where((row >= col) & (row < col + M), 1.0, 0.0).astype(bf16)


def segment_columns(own, following, band, hankel, scale_ref, offset_ref):
    width = scale_ref.shape[1]
    samples = own[:, :width]
    centre = jnp.sum(samples, axis=1, keepdims=True) * (1.0 / width)
    extended = jnp.concatenate([samples - centre, following[:, :width] - centre], axis=1)
    length = extended.shape[1]
    channels = extended.shape[0]
    stack = jnp.concatenate([*split3(extended), *split3(extended * extended)], axis=0)
    sums = jnp.dot(stack, band[...], preferred_element_type=f32)
    first, first_mid, first_low, second, second_mid, second_low = (
        sums[i * channels : (i + 1) * channels] for i in range(6)
    )
    mean = (first_low + first_mid + first) * (1.0 / M)
    spread = (second_low + second_mid + second) * (1.0 / M) - mean * mean
    scale = own[:, width:] / jnp.sqrt(jnp.maximum(spread, 0.0) + 1e-05)
    scale_ref[...] = scale
    offset_ref[...] = mean * scale
    for c in range(channels):
        base = jnp.broadcast_to(extended[c : c + 1, :], (LANES, length))
        base = pltpu.roll(base, length - LANES + 1, 1, stride=1, stride_axis=0).astype(bf16)
        for high in range(M // LANES):
            at = M - LANES - high * LANES
            hankel[c, at : at + LANES, :] = base[:, high * LANES : high * LANES + width]


def first_columns_kernel(
    limit, starts, excl, both, hankel, scale_ref, offset_ref, band_ref, sums_ref, spread_ref, banned, beyond
):
    width = banned.shape[1]
    columns = lax.axis_index("col") * width + lax.broadcasted_iota(jnp.int32, (QB, width), 1)
    apart = lax.broadcasted_iota(jnp.int32, (QB, width), 0) - columns
    last = jnp.where(columns > limit, 1.0, 0.0)
    for turn in range(starts.shape[0]):
        near = jnp.where(jnp.abs(apart + starts[turn]) < excl[0], 1.0, last)
        banned[turn * QB : (turn + 1) * QB, :] = near
    beyond[...] = last[:8]
    spread_ref[...] = spread_matrix(spread_ref.shape)
    band_ref[...] = band_matrix(band_ref.shape)
    sums_ref[...] = column_band(sums_ref.shape)
    segment_columns(both.at[0], both.at[1], sums_ref, hankel.at[0], scale_ref.at[0], offset_ref.at[0])


def second_columns_kernel(
    both, following, sums_ref, hankel_in, scale_in, offset_in, hankel, scale_ref, offset_ref
):
    segment_columns(both.at[1], following, sums_ref, hankel.at[1], scale_ref.at[1], offset_ref.at[1])


def spread_matrix(shape):
    row = lax.broadcasted_iota(jnp.int32, shape, 0)
    tile = lax.broadcasted_iota(jnp.int32, shape, 1) // LANES
    channels = shape[0] // 2
    return jnp.where((row == tile) | (row == tile + channels), 1.0, 0.0).astype(bf16)


def covariances(offsets, windows_ref, hankel, scale_ref, offset_ref, which):
    acc = -M * jnp.dot(offsets, offset_ref[which], preferred_element_type=f32, precision=lax.Precision.HIGHEST)
    for c in range(windows_ref.shape[0]):
        products = jnp.dot(windows_ref[c], hankel[which, c], preferred_element_type=f32)
        acc = acc + products * scale_ref[which, c : c + 1, :]
    return acc


def other_core_kernel(turns, y, spread_ref, hankel, scale_ref, offset_ref, out, windows_ref, scales):
    queries = turns * QB
    samples = turns * (M + QB)
    per_tile = LANES // QB
    by_query = jnp.transpose(y[:, samples : samples + queries])
    offsets = jnp.transpose(y[:, samples + queries : samples + 2 * queries])
    high = by_query.astype(bf16)
    low = (by_query - high.astype(f32)).astype(bf16)
    scales[...] = jnp.dot(jnp.concatenate([high, low], axis=1), spread_ref[...], preferred_element_type=f32)
    lines = []
    for turn in range(turns):
        at = turns * M + (turn // per_tile) * LANES
        tail = y[:, at : at + LANES]
        if turn % per_tile:
            tail = pltpu.roll(tail, LANES - (turn % per_tile) * QB, 1)
        lines.append(jnp.concatenate([y[:, turn * M : (turn + 1) * M], tail], axis=1))
    which = 1 - lax.rem(lax.axis_index("col"), CORES)
    acc = -M * jnp.dot(offsets, offset_ref[which], preferred_element_type=f32, precision=lax.Precision.HIGHEST)
    for c in range(y.shape[0]):
        windows = []
        for turn in range(turns):
            row = jnp.broadcast_to(lines[turn][c : c + 1, :], (QB, M + LANES))
            row = pltpu.roll(row, M + LANES - QB, 1, stride=1, stride_axis=0)
            scale = scales[turn * QB : (turn + 1) * QB, c * LANES : (c + 1) * LANES]
            scaled = [row[:, k : k + LANES] * scale for k in range(0, M, LANES)]
            windows.append(jnp.concatenate(scaled, axis=1).astype(bf16))
        windows = jnp.concatenate(windows, axis=0)
        windows_ref[c] = windows
        products = jnp.dot(windows, hankel[which, c], preferred_element_type=f32)
        acc = acc + products * scale_ref[which, c : c + 1, :]
    out[...] = acc


def own_core_kernel(turns, y, windows_ref, hankel, scale_ref, offset_ref, out):
    queries = turns * QB
    at = turns * (M + QB) + queries
    offsets = jnp.transpose(y[:, at : at + queries])
    which = lax.rem(lax.axis_index("col"), CORES)
    out[...] = covariances(offsets, windows_ref, hankel, scale_ref, offset_ref, which)


def minima_kernel(turns, channels, own, other, banned, beyond, row_out, col_out):
    distance = 1.0 - (own[...] + other[...]) * (1.0 / (M * channels))
    distance = jnp.where(banned[...] > 0.0, 4.0, distance)
    width = distance.shape[1]
    column_min = jnp.min(distance, axis=0, keepdims=True)
    col_out[...] = jnp.where(beyond[:1, :] > 0.0, 0.0, column_min)
    narrow = distance[:, :LANES]
    for at in range(LANES, width, LANES):
        narrow = jnp.minimum(narrow, distance[:, at : at + LANES])
    flat = jnp.min(jnp.transpose(narrow), axis=0, keepdims=True)
    for turn in range(turns):
        row_out[turn : turn + 1, :] = flat[:, turn * QB : (turn + 1) * QB]


SPECS = dict(
    v=pl.BlockSpec(memory_space=pltpu.VMEM), s=pl.BlockSpec(memory_space=pltpu.SMEM), a=pl.BlockSpec(memory_space=pl.ANY)
)


def call(kernel, name, out_shape, spaces, *operands, flops=10**6, **options):
    many = isinstance(out_shape, list)
    return pl.pallas_call(
        kernel,
        out_shape=out_shape,
        in_specs=[SPECS[space] for space in spaces],
        out_specs=[SPECS["v"]] * len(out_shape) if many else SPECS["v"],
        compiler_params=pltpu.CompilerParams(vmem_limit_bytes=40 * 2**20),
        cost_estimate=pl.CostEstimate(flops=flops, bytes_accessed=2**20, transcendentals=0),
        name=name,
        **options,
    )(*operands)


def shards(series, valid, owners, blocks, excl):
    channels, seg_len = series.shape
    devices_col = lax.axis_size("col")
    turns = owners.shape[0]
    half = channels // CORES
    queries = turns * QB
    limit = seg_len * devices_col - M
    starts = owners * seg_len + blocks * QB
    starts_vector = jnp.broadcast_to(starts.astype(f32)[:, None], (turns, LANES))

    which = lax.broadcasted_iota(jnp.int32, (2, *series.shape), 0)
    packed = jnp.where(which == 0, series[None], valid[None].astype(f32))
    part = jax.ShapeDtypeStruct((half, 2 * seg_len), f32)
    keep, send = call(share_kernel, "share", [part] * 2, "v", packed)
    chip, both = call(
        chip_kernel,
        "chip",
        [
            jax.ShapeDtypeStruct((half, 2 * seg_len + queries), f32),
            jax.ShapeDtypeStruct((CORES, half, 2 * seg_len), f32),
        ],
        "vvv",
        starts_vector,
        keep,
        exchanged(send, 1),
    )
    back = [(i, (i - CORES) % devices_col) for i in range(devices_col)]
    following = lax.ppermute(both[0, :, :seg_len], "col", back)

    side = [
        jax.ShapeDtypeStruct((CORES, half, M, seg_len), bf16),
        jax.ShapeDtypeStruct((CORES, half, seg_len), f32),
        jax.ShapeDtypeStruct((CORES, half, seg_len), f32),
    ]
    band = jax.ShapeDtypeStruct((LANES // QB * (M + QB), LANES), bf16)
    sums = jax.ShapeDtypeStruct((2 * seg_len, seg_len), bf16)
    spread = jax.ShapeDtypeStruct((2 * half, half * LANES), bf16)
    masked = [jax.ShapeDtypeStruct((queries, seg_len), f32), jax.ShapeDtypeStruct((8, seg_len), f32)]
    *columns, band, sums, spread, banned, beyond = call(
        functools.partial(first_columns_kernel, limit),
        "columns",
        [*side, band, sums, spread, *masked],
        "ssv",
        starts,
        excl,
        both,
        flops=10**8,
    )

    rounds = rounds_from(BASE, devices_col)
    masks = [0, *rounds[0]]
    total = call(
        functools.partial(windows_kernel, masks),
        "windows",
        jax.ShapeDtypeStruct((half, turns * (M + 2 * QB)), f32),
        "vaa" + "v" * len(masks),
        starts_vector,
        columns[1],
        following,
        chip,
        *[exchanged(chip, mask) for mask in rounds[0]],
        scratch_shapes=[pltpu.VMEM(((CORES * len(masks) + 1) * half, seg_len), f32)],
    )
    for others in rounds[1:]:
        total = sum([exchanged(total, mask) for mask in others], total)
    columns = call(
        second_columns_kernel,
        "columns",
        side,
        "vvvaaa",
        both,
        following,
        sums,
        *columns,
        input_output_aliases={3: 0, 4: 1, 5: 2},
        flops=10**8,
    )
    queried = call(
        functools.partial(query_kernel, turns),
        "query_stats",
        jax.ShapeDtypeStruct((half, turns * (M + 3 * QB)), f32),
        "avvv",
        columns[1],
        band,
        total,
        exchanged(total, CORES),
    )
    partial = jax.ShapeDtypeStruct((queries, seg_len), f32)
    theirs, windows = call(
        functools.partial(other_core_kernel, turns),
        "other_core",
        [partial, jax.ShapeDtypeStruct((half, queries, M), bf16)],
        "vvvvv",
        queried,
        spread,
        *columns,
        scratch_shapes=[pltpu.VMEM((queries, half * LANES), f32)],
    )
    mine = call(
        functools.partial(own_core_kernel, turns),
        "own_core",
        partial,
        "vvvvv",
        queried,
        windows,
        *columns,
        flops=5 * 10**8,
    )
    rows, column = call(
        functools.partial(minima_kernel, turns, channels),
        "minima",
        [jax.ShapeDtypeStruct((turns, QB), f32), jax.ShapeDtypeStruct((1, seg_len), f32)],
        "vvvv",
        mine,
        exchanged(theirs, 1),
        banned,
        beyond,
    )
    crossed = [[mask + 1 for mask in (others[0], *reversed(others[1:]))] for others in rounds]
    for others in [[1], [3], *crossed]:
        rows = functools.reduce(jnp.minimum, [exchanged(rows, mask) for mask in others], rows)
    return (rows, column.reshape(seg_len))


def solution(mesh):
    return jax.shard_map(
        shards,
        mesh=mesh,
        in_specs=(P(None, ("grp", "col")), P(None, ("grp", "col")), P("grp"), P("grp"), P("grp")),
        out_specs=(P("grp", None), P(("grp", "col"))),
        check_vma=False,
    )
```

```python
import functools

import jax
import jax.numpy as jnp
from jax import lax
from jax.experimental import pallas as pl
from jax.experimental.pallas import tpu as pltpu
from jax.sharding import PartitionSpec as P

M = 256
QB = 32
CORES = 2
BASE = 4
SHARE_LIMIT = 56381931
LANES = 128

f32 = jnp.float32
bf16 = jnp.bfloat16


def exchanged(block, mask):
    devices = range(lax.axis_size("col"))
    return lax.ppermute(block, "col", [(i, i ^ mask) for i in devices])


def rounds_from(base, devices):
    rounds = []
    while base < devices:
        radix = 4 if (devices // base) % 4 == 0 else 2
        rounds.append([base * i for i in range(1, radix)])
        base *= radix
    return rounds


def split3(value):
    high = value.astype(bf16)
    rest = value - high.astype(f32)
    mid = rest.astype(bf16)
    low = (rest - mid.astype(f32)).astype(bf16)
    return high, mid, low


def half_rows(ref, which):
    half = ref.shape[0]
    return pl.ds(pl.multiple_of(which * half, half), half)


def share_kernel(series, valid, keep, send, samples, flags, sems):
    copies = [
        pltpu.make_async_copy(source, target, sems.at[i])
        for i, (source, target) in enumerate([(series, samples), (valid, flags)])
    ]
    for copy in copies:
        copy.start()
    for copy in copies:
        copy.wait()
    core = lax.rem(lax.axis_index("col"), CORES)
    width = samples.shape[1]
    for which, out in ((core, keep), (1 - core, send)):
        out[:, :width] = samples[half_rows(out, which), :]
        out[:, width:] = flags[half_rows(out, which), :].astype(f32)


def first_lane(ref):
    return [jnp.max(ref[row : row + 1, :]).astype(jnp.int32) for row in range(ref.shape[0])]


def chip_kernel(starts_ref, own, other, out, both):
    turns = starts_ref.shape[0]
    starts = first_lane(starts_ref)
    half, width = own.shape[0], own.shape[1] // 2
    here = lax.axis_index("col")
    core = lax.rem(here, CORES)
    row = lax.broadcasted_iota(jnp.int32, (width, width), 0)
    col = lax.broadcasted_iota(jnp.int32, (width, width), 1)
    flip = (row + col == width - 1).astype(bf16)
    stack = jnp.concatenate(split3(own[:, :width]) + split3(other[:, :width]), axis=0)
    turned = jnp.dot(stack, flip, preferred_element_type=f32)
    for i in range(CORES):
        high, mid, low = (turned[(3 * i + j) * half : (3 * i + j + 1) * half] for j in range(3))
        out[:, i * width : (i + 1) * width] = low + mid + high
    both[core] = own[...]
    both[1 - core] = other[...]
    lane = lax.broadcasted_iota(jnp.int32, (half, LANES), 1)
    per_tile = LANES // QB
    for tile in range(turns // per_tile):
        valids = jnp.zeros((half, LANES), f32)
        for i in range(per_tile):
            start = starts[tile * per_tile + i]
            owner, shift = start // width, lax.rem(start, width)
            mine = (owner == here).astype(f32)
            others = (owner == here ^ 1).astype(f32)
            flags = mine * own[:, width:] + others * other[:, width:]
            flags = pltpu.roll(flags, lax.rem(width - shift, width), 1)[:, :LANES]
            if i:
                flags = pltpu.roll(flags, i * QB, 1)
            valids = jnp.where((lane >= i * QB) & (lane < (i + 1) * QB), flags, valids)
        at = 2 * width + tile * LANES
        out[:, at : at + LANES] = valids


def windows_kernel(masks, starts_ref, after, after_too, *refs):
    parts, out, lines = refs[: len(masks)], refs[len(masks)], refs[len(masks) + 1]
    turns = starts_ref.shape[0]
    starts = first_lane(starts_ref)
    half, width = out.shape[0], lines.shape[1]
    here = lax.axis_index("col")
    for i, part in enumerate(parts):
        for j in range(CORES):
            at = (CORES * i + j) * half
            lines[at : at + half, :] = part[:, j * width : (j + 1) * width]
    none = CORES * len(masks)
    lines[none * half :, :] = jnp.zeros((half, width), f32)
    held = sum(masks[i] for i in range(1, len(masks)) if masks[i] & (masks[i] - 1) == 0) + CORES - 1

    def segment(device):
        relative = device ^ here
        slot = CORES * ((relative & (held - CORES + 1)) // BASE) + (relative & (CORES - 1))
        slot = jnp.where((relative & held) == relative, slot, none)
        return lines[pl.ds(pl.multiple_of(slot * half, half), half), :]

    lane = lax.broadcasted_iota(jnp.int32, (half, width), 1)
    lane_128 = lax.broadcasted_iota(jnp.int32, (half, LANES), 1)
    per_tile = LANES // QB
    for tile in range(turns // per_tile):
        tails = jnp.zeros((half, LANES), f32)
        for i in range(per_tile):
            turn = tile * per_tile + i
            owner, split = starts[turn] // width, lax.rem(starts[turn], width) + QB
            amount = lax.rem(split, width)
            first = pltpu.roll(segment(owner), amount, 1)
            second = pltpu.roll(segment(owner + 1), amount, 1)
            out[:, turn * M : (turn + 1) * M] = jnp.where(lane >= split, first, second)
            tail = first[:, :LANES]
            if i:
                tail = pltpu.roll(tail, i * QB, 1)
            tails = jnp.where((lane_128 >= i * QB) & (lane_128 < (i + 1) * QB), tail, tails)
        at = turns * M + tile * LANES
        out[:, at : at + LANES] = tails
        at = turns * (M + QB) + tile * LANES
        flags = slice(2 * width + tile * LANES, 2 * width + (tile + 1) * LANES)
        out[:, at : at + LANES] = sum([part[:, flags] for part in parts[1:]], parts[0][:, flags])


def query_kernel(turns, after, band_ref, *refs):
    parts, out = refs[:-1], refs[-1]
    total = parts[0][...]
    for part in parts[1:]:
        total = total + part[...]
    samples = turns * (M + QB)
    per_tile = LANES // QB
    main, tail = [], []
    for tile in range(turns // per_tile):
        at = turns * M + tile * LANES
        tail_tile = total[:, at : at + LANES]
        lane = lax.broadcasted_iota(jnp.int32, tail_tile.shape, 1)
        centre = jnp.zeros_like(tail_tile)
        for i in range(per_tile):
            turn = tile * per_tile + i
            block = total[:, turn * M : (turn + 1) * M]
            mean = jnp.sum(block, axis=1, keepdims=True) * (1.0 / M)
            main.append(block - mean)
            centre = jnp.where((lane >= i * QB) & (lane < (i + 1) * QB), mean, centre)
        tail.append(tail_tile - centre)
    for tile in range(turns // per_tile):
        rows = main[tile * per_tile : (tile + 1) * per_tile] + [tail[tile]]
        shifted = jnp.concatenate(rows, axis=1)
        half = shifted.shape[0]
        stack = jnp.concatenate([*split3(shifted), *split3(shifted * shifted)], axis=0)
        sums = jnp.dot(stack, band_ref[...], preferred_element_type=f32)
        first = sums[2 * half : 3 * half] + sums[half : 2 * half] + sums[:half]
        second = sums[5 * half : 6 * half] + sums[4 * half : 5 * half] + sums[3 * half : 4 * half]
        mean = first * (1.0 / M)
        spread = second * (1.0 / M) - mean * mean
        at = samples + tile * LANES
        scale = total[:, at : at + LANES] / jnp.sqrt(spread + 1e-05)
        out[:, at : at + LANES] = scale
        out[:, at + turns * QB : at + turns * QB + LANES] = mean * scale
    for turn in range(turns):
        out[:, turn * M : (turn + 1) * M] = main[turn]
    for tile in range(turns // per_tile):
        at = turns * M + tile * LANES
        out[:, at : at + LANES] = tail[tile]


def band_matrix(shape):
    lane = lax.broadcasted_iota(jnp.int32, shape, 0)
    query = lax.broadcasted_iota(jnp.int32, shape, 1)
    per_tile = LANES // QB
    beyond = lane - per_tile * M
    turn = jnp.where(beyond < 0, lane // M, beyond // QB)
    place = jnp.where(beyond < 0, lane % M, M + beyond % QB)
    q = query % QB
    inside = (turn == query // QB) & (place >= QB - q) & (place <= M + QB - 1 - q)
    return jnp.where(inside, 1.0, 0.0).astype(bf16)


def column_band(shape):
    row = lax.broadcasted_iota(jnp.int32, shape, 0)
    col = lax.broadcasted_iota(jnp.int32, shape, 1)
    return jnp.where((row >= col) & (row < col + M), 1.0, 0.0).astype(bf16)


def segment_columns(own, following, band, hankel, scale_ref, offset_ref):
    width = scale_ref.shape[1]
    samples = own[:, :width]
    centre = jnp.sum(samples, axis=1, keepdims=True) * (1.0 / width)
    extended = jnp.concatenate([samples - centre, following[:, :width] - centre], axis=1)
    length = extended.shape[1]
    channels = extended.shape[0]
    stack = jnp.concatenate([*split3(extended), *split3(extended * extended)], axis=0)
    sums = jnp.dot(stack, band[...], preferred_element_type=f32)
    first, first_mid, first_low, second, second_mid, second_low = (
        sums[i * channels : (i + 1) * channels] for i in range(6)
    )
    mean = (first_low + first_mid + first) * (1.0 / M)
    spread = (second_low + second_mid + second) * (1.0 / M) - mean * mean
    scale = own[:, width:] / jnp.sqrt(jnp.maximum(spread, 0.0) + 1e-05)
    scale_ref[...] = scale
    offset_ref[...] = mean * scale
    for c in range(channels):
        base = jnp.broadcast_to(extended[c : c + 1, :], (LANES, length))
        base = pltpu.roll(base, length - LANES + 1, 1, stride=1, stride_axis=0).astype(bf16)
        for high in range(M // LANES):
            at = M - LANES - high * LANES
            hankel[c, at : at + LANES, :] = base[:, high * LANES : high * LANES + width]


def first_columns_kernel(
    limit, starts, excl, both, hankel, scale_ref, offset_ref, band_ref, sums_ref, spread_ref, banned, beyond
):
    width = banned.shape[1]
    columns = lax.axis_index("col") * width + lax.broadcasted_iota(jnp.int32, (QB, width), 1)
    apart = lax.broadcasted_iota(jnp.int32, (QB, width), 0) - columns
    last = jnp.where(columns > limit, 1.0, 0.0)
    for turn in range(starts.shape[0]):
        near = jnp.where(jnp.abs(apart + starts[turn]) < excl[0], 1.0, last)
        banned[turn * QB : (turn + 1) * QB, :] = near
    beyond[...] = last[:8]
    spread_ref[...] = spread_matrix(spread_ref.shape)
    band_ref[...] = band_matrix(band_ref.shape)
    sums_ref[...] = column_band(sums_ref.shape)
    segment_columns(both.at[0], both.at[1], sums_ref, hankel.at[0], scale_ref.at[0], offset_ref.at[0])


def second_columns_kernel(
    both, following, sums_ref, hankel_in, scale_in, offset_in, hankel, scale_ref, offset_ref
):
    segment_columns(both.at[1], following, sums_ref, hankel.at[1], scale_ref.at[1], offset_ref.at[1])


def spread_matrix(shape):
    row = lax.broadcasted_iota(jnp.int32, shape, 0)
    tile = lax.broadcasted_iota(jnp.int32, shape, 1) // LANES
    channels = shape[0] // 2
    return jnp.where((row == tile) | (row == tile + channels), 1.0, 0.0).astype(bf16)


def covariances(offsets, windows_ref, hankel, scale_ref, offset_ref, which):
    acc = -M * jnp.dot(offsets, offset_ref[which], preferred_element_type=f32, precision=lax.Precision.HIGHEST)
    for c in range(windows_ref.shape[0]):
        products = jnp.dot(windows_ref[c], hankel[which, c], preferred_element_type=f32)
        acc = acc + products * scale_ref[which, c : c + 1, :]
    return acc


def other_core_kernel(turns, y, spread_ref, hankel, scale_ref, offset_ref, out, windows_ref, scales):
    queries = turns * QB
    samples = turns * (M + QB)
    per_tile = LANES // QB
    by_query = jnp.transpose(y[:, samples : samples + queries])
    offsets = jnp.transpose(y[:, samples + queries : samples + 2 * queries])
    high = by_query.astype(bf16)
    low = (by_query - high.astype(f32)).astype(bf16)
    scales[...] = jnp.dot(jnp.concatenate([high, low], axis=1), spread_ref[...], preferred_element_type=f32)
    lines = []
    for turn in range(turns):
        at = turns * M + (turn // per_tile) * LANES
        tail = y[:, at : at + LANES]
        if turn % per_tile:
            tail = pltpu.roll(tail, LANES - (turn % per_tile) * QB, 1)
        lines.append(jnp.concatenate([y[:, turn * M : (turn + 1) * M], tail], axis=1))
    which = 1 - lax.rem(lax.axis_index("col"), CORES)
    acc = -M * jnp.dot(offsets, offset_ref[which], preferred_element_type=f32, precision=lax.Precision.HIGHEST)
    for c in range(y.shape[0]):
        windows = []
        for turn in range(turns):
            row = jnp.broadcast_to(lines[turn][c : c + 1, :], (QB, M + LANES))
            row = pltpu.roll(row, M + LANES - QB, 1, stride=1, stride_axis=0)
            scale = scales[turn * QB : (turn + 1) * QB, c * LANES : (c + 1) * LANES]
            scaled = [row[:, k : k + LANES] * scale for k in range(0, M, LANES)]
            windows.append(jnp.concatenate(scaled, axis=1).astype(bf16))
        windows = jnp.concatenate(windows, axis=0)
        windows_ref[c] = windows
        products = jnp.dot(windows, hankel[which, c], preferred_element_type=f32)
        acc = acc + products * scale_ref[which, c : c + 1, :]
    out[...] = acc


def own_core_kernel(turns, y, windows_ref, hankel, scale_ref, offset_ref, out):
    queries = turns * QB
    at = turns * (M + QB) + queries
    offsets = jnp.transpose(y[:, at : at + queries])
    which = lax.rem(lax.axis_index("col"), CORES)
    out[...] = covariances(offsets, windows_ref, hankel, scale_ref, offset_ref, which)


def minima_kernel(turns, channels, own, other, banned, beyond, row_out, col_out):
    distance = 1.0 - (own[...] + other[...]) * (1.0 / (M * channels))
    distance = jnp.where(banned[...] > 0.0, 4.0, distance)
    width = distance.shape[1]
    column_min = jnp.min(distance, axis=0, keepdims=True)
    col_out[...] = jnp.where(beyond[:1, :] > 0.0, 0.0, column_min)
    narrow = distance[:, :LANES]
    for at in range(LANES, width, LANES):
        narrow = jnp.minimum(narrow, distance[:, at : at + LANES])
    flat = jnp.min(jnp.transpose(narrow), axis=0, keepdims=True)
    for turn in range(turns):
        row_out[turn : turn + 1, :] = flat[:, turn * QB : (turn + 1) * QB]


SPECS = dict(
    v=pl.BlockSpec(memory_space=pltpu.VMEM), s=pl.BlockSpec(memory_space=pltpu.SMEM), a=pl.BlockSpec(memory_space=pl.ANY)
)


def call(kernel, name, out_shape, spaces, *operands, flops=10**6, limit=40 * 2**20, **options):
    many = isinstance(out_shape, list)
    return pl.pallas_call(
        kernel,
        out_shape=out_shape,
        in_specs=[SPECS[space] for space in spaces],
        out_specs=[SPECS["v"]] * len(out_shape) if many else SPECS["v"],
        compiler_params=pltpu.CompilerParams(vmem_limit_bytes=limit),
        cost_estimate=pl.CostEstimate(flops=flops, bytes_accessed=2**20, transcendentals=0),
        name=name,
        **options,
    )(*operands)


def shards(series, valid, owners, blocks, excl):
    channels, seg_len = series.shape
    devices_col = lax.axis_size("col")
    turns = owners.shape[0]
    half = channels // CORES
    queries = turns * QB
    limit = seg_len * devices_col - M
    starts = owners * seg_len + blocks * QB
    starts_vector = jnp.broadcast_to(starts.astype(f32)[:, None], (turns, LANES))

    part = jax.ShapeDtypeStruct((half, 2 * seg_len), f32)
    keep, send = call(
        share_kernel,
        "share",
        [part] * 2,
        "aa",
        series,
        valid,
        scratch_shapes=[
            pltpu.VMEM(series.shape, f32),
            pltpu.VMEM(valid.shape, jnp.int32),
            pltpu.SemaphoreType.DMA((2,)),
        ],
        limit=SHARE_LIMIT,
    )
    chip, both = call(
        chip_kernel,
        "chip",
        [
            jax.ShapeDtypeStruct((half, 2 * seg_len + queries), f32),
            jax.ShapeDtypeStruct((CORES, half, 2 * seg_len), f32),
        ],
        "vvv",
        starts_vector,
        keep,
        exchanged(send, 1),
    )
    back = [(i, (i - CORES) % devices_col) for i in range(devices_col)]
    following = lax.ppermute(both[0, :, :seg_len], "col", back)

    side = [
        jax.ShapeDtypeStruct((CORES, half, M, seg_len), bf16),
        jax.ShapeDtypeStruct((CORES, half, seg_len), f32),
        jax.ShapeDtypeStruct((CORES, half, seg_len), f32),
    ]
    band = jax.ShapeDtypeStruct((LANES // QB * (M + QB), LANES), bf16)
    sums = jax.ShapeDtypeStruct((2 * seg_len, seg_len), bf16)
    spread = jax.ShapeDtypeStruct((2 * half, half * LANES), bf16)
    masked = [jax.ShapeDtypeStruct((queries, seg_len), f32), jax.ShapeDtypeStruct((8, seg_len), f32)]
    *columns, band, sums, spread, banned, beyond = call(
        functools.partial(first_columns_kernel, limit),
        "columns",
        [*side, band, sums, spread, *masked],
        "ssv",
        starts,
        excl,
        both,
        flops=10**8,
    )

    rounds = rounds_from(BASE, devices_col)
    masks = [0, *rounds[0]]
    total = call(
        functools.partial(windows_kernel, masks),
        "windows",
        jax.ShapeDtypeStruct((half, turns * (M + 2 * QB)), f32),
        "vaa" + "v" * len(masks),
        starts_vector,
        columns[1],
        following,
        chip,
        *[exchanged(chip, mask) for mask in rounds[0]],
        scratch_shapes=[pltpu.VMEM(((CORES * len(masks) + 1) * half, seg_len), f32)],
    )
    for others in rounds[1:]:
        total = sum([exchanged(total, mask) for mask in others], total)
    columns = call(
        second_columns_kernel,
        "columns",
        side,
        "vvvaaa",
        both,
        following,
        sums,
        *columns,
        input_output_aliases={3: 0, 4: 1, 5: 2},
        flops=10**8,
    )
    queried = call(
        functools.partial(query_kernel, turns),
        "query_stats",
        jax.ShapeDtypeStruct((half, turns * (M + 3 * QB)), f32),
        "avvv",
        columns[1],
        band,
        total,
        exchanged(total, CORES),
    )
    partial = jax.ShapeDtypeStruct((queries, seg_len), f32)
    theirs, windows = call(
        functools.partial(other_core_kernel, turns),
        "other_core",
        [partial, jax.ShapeDtypeStruct((half, queries, M), bf16)],
        "vvvvv",
        queried,
        spread,
        *columns,
        scratch_shapes=[pltpu.VMEM((queries, half * LANES), f32)],
    )
    mine = call(
        functools.partial(own_core_kernel, turns),
        "own_core",
        partial,
        "vvvvv",
        queried,
        windows,
        *columns,
        flops=5 * 10**8,
    )
    rows, column = call(
        functools.partial(minima_kernel, turns, channels),
        "minima",
        [jax.ShapeDtypeStruct((turns, QB), f32), jax.ShapeDtypeStruct((1, seg_len), f32)],
        "vvvv",
        mine,
        exchanged(theirs, 1),
        banned,
        beyond,
    )
    crossed = [[mask + 1 for mask in (others[0], *reversed(others[1:]))] for others in rounds]
    for others in [[1], [3], *crossed]:
        rows = functools.reduce(jnp.minimum, [exchanged(rows, mask) for mask in others], rows)
    return (rows, column.reshape(seg_len))


def solution(mesh):
    return jax.shard_map(
        shards,
        mesh=mesh,
        in_specs=(P(None, ("grp", "col")), P(None, ("grp", "col")), P("grp"), P("grp"), P("grp")),
        out_specs=(P("grp", None), P(("grp", "col"))),
        check_vma=False,
    )
```

```python
import functools

import jax
import jax.numpy as jnp
from jax import lax
from jax.experimental import pallas as pl
from jax.experimental.pallas import tpu as pltpu
from jax.sharding import PartitionSpec as P

M = 256
QB = 32
CORES = 2
BASE = 4
SHARE_LIMIT = 56381931
LANES = 128

f32 = jnp.float32
bf16 = jnp.bfloat16


def exchanged(block, mask):
    devices = range(lax.axis_size("col"))
    return lax.ppermute(block, "col", [(i, i ^ mask) for i in devices])


def rounds_from(base, devices):
    rounds = []
    while base < devices:
        radix = 4 if (devices // base) % 4 == 0 else 2
        rounds.append([base * i for i in range(1, radix)])
        base *= radix
    return rounds


def split3(value):
    high = value.astype(bf16)
    rest = value - high.astype(f32)
    mid = rest.astype(bf16)
    low = (rest - mid.astype(f32)).astype(bf16)
    return high, mid, low


def half_rows(ref, which):
    half = ref.shape[0]
    return pl.ds(pl.multiple_of(which * half, half), half)


def share_kernel(series, valid, keep, send, samples, flags, sems):
    copies = [
        pltpu.make_async_copy(source, target, sems.at[i])
        for i, (source, target) in enumerate([(series, samples), (valid, flags)])
    ]
    for copy in copies:
        copy.start()
    for copy in copies:
        copy.wait()
    core = lax.rem(lax.axis_index("col"), CORES)
    width = samples.shape[1]
    for which, out in ((core, keep), (1 - core, send)):
        out[:, :width] = samples[half_rows(out, which), :]
        out[:, width:] = flags[half_rows(out, which), :].astype(f32)


def first_lane(ref):
    return [jnp.max(ref[row : row + 1, :]).astype(jnp.int32) for row in range(ref.shape[0])]


def chip_kernel(starts_ref, own, other, out, both):
    turns = starts_ref.shape[0]
    starts = first_lane(starts_ref)
    half, width = own.shape[0], own.shape[1] // 2
    here = lax.axis_index("col")
    core = lax.rem(here, CORES)
    row = lax.broadcasted_iota(jnp.int32, (width, width), 0)
    col = lax.broadcasted_iota(jnp.int32, (width, width), 1)
    flip = (row + col == width - 1).astype(bf16)
    stack = jnp.concatenate(split3(own[:, :width]) + split3(other[:, :width]), axis=0)
    turned = jnp.dot(stack, flip, preferred_element_type=f32)
    for i in range(CORES):
        high, mid, low = (turned[(3 * i + j) * half : (3 * i + j + 1) * half] for j in range(3))
        out[:, i * width : (i + 1) * width] = low + mid + high
    both[core] = own[...]
    both[1 - core] = other[...]
    lane = lax.broadcasted_iota(jnp.int32, (half, LANES), 1)
    per_tile = LANES // QB
    for tile in range(turns // per_tile):
        valids = jnp.zeros((half, LANES), f32)
        for i in range(per_tile):
            start = starts[tile * per_tile + i]
            owner, shift = start // width, lax.rem(start, width)
            mine = (owner == here).astype(f32)
            others = (owner == here ^ 1).astype(f32)
            flags = mine * own[:, width:] + others * other[:, width:]
            flags = pltpu.roll(flags, lax.rem(width - shift, width), 1)[:, :LANES]
            if i:
                flags = pltpu.roll(flags, i * QB, 1)
            valids = jnp.where((lane >= i * QB) & (lane < (i + 1) * QB), flags, valids)
        at = 2 * width + tile * LANES
        out[:, at : at + LANES] = valids


def windows_kernel(masks, starts_ref, after, after_too, *refs):
    parts, out, lines = refs[: len(masks)], refs[len(masks)], refs[len(masks) + 1]
    turns = starts_ref.shape[0]
    starts = first_lane(starts_ref)
    half, width = out.shape[0], lines.shape[1]
    here = lax.axis_index("col")
    for i, part in enumerate(parts):
        for j in range(CORES):
            at = (CORES * i + j) * half
            lines[at : at + half, :] = part[:, j * width : (j + 1) * width]
    none = CORES * len(masks)
    lines[none * half :, :] = jnp.zeros((half, width), f32)
    held = sum(masks[i] for i in range(1, len(masks)) if masks[i] & (masks[i] - 1) == 0) + CORES - 1

    def segment(device):
        relative = device ^ here
        slot = CORES * ((relative & (held - CORES + 1)) // BASE) + (relative & (CORES - 1))
        slot = jnp.where((relative & held) == relative, slot, none)
        return lines[pl.ds(pl.multiple_of(slot * half, half), half), :]

    lane = lax.broadcasted_iota(jnp.int32, (half, width), 1)
    lane_128 = lax.broadcasted_iota(jnp.int32, (half, LANES), 1)
    per_tile = LANES // QB
    for tile in range(turns // per_tile):
        tails = jnp.zeros((half, LANES), f32)
        for i in range(per_tile):
            turn = tile * per_tile + i
            owner, split = starts[turn] // width, lax.rem(starts[turn], width) + QB
            amount = lax.rem(split, width)
            first = pltpu.roll(segment(owner), amount, 1)
            second = pltpu.roll(segment(owner + 1), amount, 1)
            out[:, turn * M : (turn + 1) * M] = jnp.where(lane >= split, first, second)
            tail = first[:, :LANES]
            if i:
                tail = pltpu.roll(tail, i * QB, 1)
            tails = jnp.where((lane_128 >= i * QB) & (lane_128 < (i + 1) * QB), tail, tails)
        at = turns * M + tile * LANES
        out[:, at : at + LANES] = tails
        at = turns * (M + QB) + tile * LANES
        flags = slice(2 * width + tile * LANES, 2 * width + (tile + 1) * LANES)
        out[:, at : at + LANES] = sum([part[:, flags] for part in parts[1:]], parts[0][:, flags])


def query_kernel(turns, after, band_ref, *refs):
    parts, out = refs[:-1], refs[-1]
    total = parts[0][...]
    for part in parts[1:]:
        total = total + part[...]
    samples = turns * (M + QB)
    per_tile = LANES // QB
    main, tail = [], []
    for tile in range(turns // per_tile):
        at = turns * M + tile * LANES
        tail_tile = total[:, at : at + LANES]
        lane = lax.broadcasted_iota(jnp.int32, tail_tile.shape, 1)
        centre = jnp.zeros_like(tail_tile)
        for i in range(per_tile):
            turn = tile * per_tile + i
            block = total[:, turn * M : (turn + 1) * M]
            mean = jnp.sum(block, axis=1, keepdims=True) * (1.0 / M)
            main.append(block - mean)
            centre = jnp.where((lane >= i * QB) & (lane < (i + 1) * QB), mean, centre)
        tail.append(tail_tile - centre)
    for tile in range(turns // per_tile):
        rows = main[tile * per_tile : (tile + 1) * per_tile] + [tail[tile]]
        shifted = jnp.concatenate(rows, axis=1)
        half = shifted.shape[0]
        stack = jnp.concatenate([*split3(shifted), *split3(shifted * shifted)], axis=0)
        sums = jnp.dot(stack, band_ref[...], preferred_element_type=f32)
        first = sums[2 * half : 3 * half] + sums[half : 2 * half] + sums[:half]
        second = sums[5 * half : 6 * half] + sums[4 * half : 5 * half] + sums[3 * half : 4 * half]
        mean = first * (1.0 / M)
        spread = second * (1.0 / M) - mean * mean
        at = samples + tile * LANES
        scale = total[:, at : at + LANES] / jnp.sqrt(spread + 1e-05)
        out[:, at : at + LANES] = scale
        out[:, at + turns * QB : at + turns * QB + LANES] = mean * scale
    for turn in range(turns):
        out[:, turn * M : (turn + 1) * M] = main[turn]
    for tile in range(turns // per_tile):
        at = turns * M + tile * LANES
        out[:, at : at + LANES] = tail[tile]


def band_matrix(shape):
    lane = lax.broadcasted_iota(jnp.int32, shape, 0)
    query = lax.broadcasted_iota(jnp.int32, shape, 1)
    per_tile = LANES // QB
    beyond = lane - per_tile * M
    turn = jnp.where(beyond < 0, lane // M, beyond // QB)
    place = jnp.where(beyond < 0, lane % M, M + beyond % QB)
    q = query % QB
    inside = (turn == query // QB) & (place >= QB - q) & (place <= M + QB - 1 - q)
    return jnp.where(inside, 1.0, 0.0).astype(bf16)


def column_band(shape):
    row = lax.broadcasted_iota(jnp.int32, shape, 0)
    col = lax.broadcasted_iota(jnp.int32, shape, 1)
    return jnp.where((row >= col) & (row < col + M), 1.0, 0.0).astype(bf16)


def segment_columns(own, following, band, hankel, scale_ref, offset_ref):
    width = scale_ref.shape[1]
    samples = own[:, :width]
    centre = jnp.sum(samples, axis=1, keepdims=True) * (1.0 / width)
    extended = jnp.concatenate([samples - centre, following[:, :width] - centre], axis=1)
    length = extended.shape[1]
    channels = extended.shape[0]
    stack = jnp.concatenate([*split3(extended), *split3(extended * extended)], axis=0)
    sums = jnp.dot(stack, band[...], preferred_element_type=f32)
    first, first_mid, first_low, second, second_mid, second_low = (
        sums[i * channels : (i + 1) * channels] for i in range(6)
    )
    mean = (first_low + first_mid + first) * (1.0 / M)
    spread = (second_low + second_mid + second) * (1.0 / M) - mean * mean
    scale = own[:, width:] / jnp.sqrt(jnp.maximum(spread, 0.0) + 1e-05)
    scale_ref[...] = scale
    offset_ref[...] = mean * scale
    for c in range(channels):
        base = jnp.broadcast_to(extended[c : c + 1, :], (LANES, length))
        base = pltpu.roll(base, length - LANES + 1, 1, stride=1, stride_axis=0).astype(bf16)
        for high in range(M // LANES):
            at = M - LANES - high * LANES
            hankel[c, at : at + LANES, :] = base[:, high * LANES : high * LANES + width]


def first_columns_kernel(
    limit, starts, excl, both, hankel, scale_ref, offset_ref, band_ref, sums_ref, spread_ref, banned, beyond
):
    width = beyond.shape[1]
    here = lax.axis_index("col")
    for i in range(CORES):
        columns = (here ^ i) * width + lax.broadcasted_iota(jnp.int32, (QB, width), 1)
        apart = lax.broadcasted_iota(jnp.int32, (QB, width), 0) - columns
        last = jnp.where(columns > limit, 1.0, 0.0)
        for turn in range(starts.shape[0]):
            near = jnp.where(jnp.abs(apart + starts[turn]) < excl[0], 1.0, last)
            banned[i, turn * QB : (turn + 1) * QB, :] = near
        if i == 0:
            beyond[...] = last[:8]
    spread_ref[...] = spread_matrix(spread_ref.shape)
    band_ref[...] = band_matrix(band_ref.shape)
    sums_ref[...] = column_band(sums_ref.shape)
    segment_columns(both.at[0], both.at[1], sums_ref, hankel.at[0], scale_ref.at[0], offset_ref.at[0])


def second_columns_kernel(
    both, following, sums_ref, hankel_in, scale_in, offset_in, hankel, scale_ref, offset_ref
):
    segment_columns(both.at[1], following, sums_ref, hankel.at[1], scale_ref.at[1], offset_ref.at[1])


def spread_matrix(shape):
    row = lax.broadcasted_iota(jnp.int32, shape, 0)
    tile = lax.broadcasted_iota(jnp.int32, shape, 1) // LANES
    channels = shape[0] // 2
    return jnp.where((row == tile) | (row == tile + channels), 1.0, 0.0).astype(bf16)


def covariances(offsets, windows_ref, hankel, scale_ref, offset_ref, which):
    acc = -M * jnp.dot(offsets, offset_ref[which], preferred_element_type=f32, precision=lax.Precision.HIGHEST)
    for c in range(windows_ref.shape[0]):
        products = jnp.dot(windows_ref[c], hankel[which, c], preferred_element_type=f32)
        acc = acc + products * scale_ref[which, c : c + 1, :]
    return acc


def other_core_kernel(turns, y, spread_ref, hankel, scale_ref, offset_ref, out, windows_ref, scales):
    queries = turns * QB
    samples = turns * (M + QB)
    per_tile = LANES // QB
    by_query = jnp.transpose(y[:, samples : samples + queries])
    offsets = jnp.transpose(y[:, samples + queries : samples + 2 * queries])
    high = by_query.astype(bf16)
    low = (by_query - high.astype(f32)).astype(bf16)
    scales[...] = jnp.dot(jnp.concatenate([high, low], axis=1), spread_ref[...], preferred_element_type=f32)
    lines = []
    for turn in range(turns):
        at = turns * M + (turn // per_tile) * LANES
        tail = y[:, at : at + LANES]
        if turn % per_tile:
            tail = pltpu.roll(tail, LANES - (turn % per_tile) * QB, 1)
        lines.append(jnp.concatenate([y[:, turn * M : (turn + 1) * M], tail], axis=1))
    which = 1 - lax.rem(lax.axis_index("col"), CORES)
    acc = -M * jnp.dot(offsets, offset_ref[which], preferred_element_type=f32, precision=lax.Precision.HIGHEST)
    for c in range(y.shape[0]):
        windows = []
        for turn in range(turns):
            row = jnp.broadcast_to(lines[turn][c : c + 1, :], (QB, M + LANES))
            row = pltpu.roll(row, M + LANES - QB, 1, stride=1, stride_axis=0)
            scale = scales[turn * QB : (turn + 1) * QB, c * LANES : (c + 1) * LANES]
            scaled = [row[:, k : k + LANES] * scale for k in range(0, M, LANES)]
            windows.append(jnp.concatenate(scaled, axis=1).astype(bf16))
        windows = jnp.concatenate(windows, axis=0)
        windows_ref[c] = windows
        products = jnp.dot(windows, hankel[which, c], preferred_element_type=f32)
        acc = acc + products * scale_ref[which, c : c + 1, :]
    out[...] = acc


def own_core_kernel(turns, y, windows_ref, hankel, scale_ref, offset_ref, out):
    queries = turns * QB
    at = turns * (M + QB) + queries
    offsets = jnp.transpose(y[:, at : at + queries])
    which = lax.rem(lax.axis_index("col"), CORES)
    out[...] = covariances(offsets, windows_ref, hankel, scale_ref, offset_ref, which)


def allowed_minima(channels, which, own, other, banned):
    distance = 1.0 - (own[...] + other[...]) * (1.0 / (M * channels))
    distance = jnp.where(banned[which] > 0.0, 4.0, distance)
    narrow = distance[:, :LANES]
    for at in range(LANES, distance.shape[1], LANES):
        narrow = jnp.minimum(narrow, distance[:, at : at + LANES])
    return distance, narrow


def own_minima_kernel(channels, own, other, banned, beyond, narrow_out, col_out):
    distance, narrow_out[...] = allowed_minima(channels, 0, own, other, banned)
    column_min = jnp.min(distance, axis=0, keepdims=True)
    col_out[...] = jnp.where(beyond[:1, :] > 0.0, 0.0, column_min)


def chip_minima_kernel(turns, channels, own, other, banned, narrow, row_out):
    _, others = allowed_minima(channels, 1, own, other, banned)
    flat = jnp.min(jnp.transpose(jnp.minimum(others, narrow[...])), axis=0, keepdims=True)
    for turn in range(turns):
        row_out[turn : turn + 1, :] = flat[:, turn * QB : (turn + 1) * QB]


SPECS = dict(
    v=pl.BlockSpec(memory_space=pltpu.VMEM), s=pl.BlockSpec(memory_space=pltpu.SMEM), a=pl.BlockSpec(memory_space=pl.ANY)
)


def call(kernel, name, out_shape, spaces, *operands, flops=10**6, limit=40 * 2**20, **options):
    many = isinstance(out_shape, list)
    return pl.pallas_call(
        kernel,
        out_shape=out_shape,
        in_specs=[SPECS[space] for space in spaces],
        out_specs=[SPECS["v"]] * len(out_shape) if many else SPECS["v"],
        compiler_params=pltpu.CompilerParams(vmem_limit_bytes=limit),
        cost_estimate=pl.CostEstimate(flops=flops, bytes_accessed=2**20, transcendentals=0),
        name=name,
        **options,
    )(*operands)


def shards(series, valid, owners, blocks, excl):
    channels, seg_len = series.shape
    devices_col = lax.axis_size("col")
    turns = owners.shape[0]
    half = channels // CORES
    queries = turns * QB
    limit = seg_len * devices_col - M
    starts = owners * seg_len + blocks * QB
    starts_vector = jnp.broadcast_to(starts.astype(f32)[:, None], (turns, LANES))

    part = jax.ShapeDtypeStruct((half, 2 * seg_len), f32)
    keep, send = call(
        share_kernel,
        "share",
        [part] * 2,
        "aa",
        series,
        valid,
        scratch_shapes=[
            pltpu.VMEM(series.shape, f32),
            pltpu.VMEM(valid.shape, jnp.int32),
            pltpu.SemaphoreType.DMA((2,)),
        ],
        limit=SHARE_LIMIT,
    )
    chip, both = call(
        chip_kernel,
        "chip",
        [
            jax.ShapeDtypeStruct((half, 2 * seg_len + queries), f32),
            jax.ShapeDtypeStruct((CORES, half, 2 * seg_len), f32),
        ],
        "vvv",
        starts_vector,
        keep,
        exchanged(send, 1),
    )
    back = [(i, (i - CORES) % devices_col) for i in range(devices_col)]
    following = lax.ppermute(both[0, :, :seg_len], "col", back)

    side = [
        jax.ShapeDtypeStruct((CORES, half, M, seg_len), bf16),
        jax.ShapeDtypeStruct((CORES, half, seg_len), f32),
        jax.ShapeDtypeStruct((CORES, half, seg_len), f32),
    ]
    band = jax.ShapeDtypeStruct((LANES // QB * (M + QB), LANES), bf16)
    sums = jax.ShapeDtypeStruct((2 * seg_len, seg_len), bf16)
    spread = jax.ShapeDtypeStruct((2 * half, half * LANES), bf16)
    masked = [jax.ShapeDtypeStruct((CORES, queries, seg_len), f32), jax.ShapeDtypeStruct((8, seg_len), f32)]
    *columns, band, sums, spread, banned, beyond = call(
        functools.partial(first_columns_kernel, limit),
        "columns",
        [*side, band, sums, spread, *masked],
        "ssv",
        starts,
        excl,
        both,
        flops=10**8,
    )

    rounds = rounds_from(BASE, devices_col)
    masks = [0, *rounds[0]]
    total = call(
        functools.partial(windows_kernel, masks),
        "windows",
        jax.ShapeDtypeStruct((half, turns * (M + 2 * QB)), f32),
        "vaa" + "v" * len(masks),
        starts_vector,
        columns[1],
        following,
        chip,
        *[exchanged(chip, mask) for mask in rounds[0]],
        scratch_shapes=[pltpu.VMEM(((CORES * len(masks) + 1) * half, seg_len), f32)],
    )
    for others in rounds[1:]:
        total = sum([exchanged(total, mask) for mask in others], total)
    columns = call(
        second_columns_kernel,
        "columns",
        side,
        "vvvaaa",
        both,
        following,
        sums,
        *columns,
        input_output_aliases={3: 0, 4: 1, 5: 2},
        flops=10**8,
    )
    queried = call(
        functools.partial(query_kernel, turns),
        "query_stats",
        jax.ShapeDtypeStruct((half, turns * (M + 3 * QB)), f32),
        "avvv",
        columns[1],
        band,
        total,
        exchanged(total, CORES),
    )
    partial = jax.ShapeDtypeStruct((queries, seg_len), f32)
    theirs, windows = call(
        functools.partial(other_core_kernel, turns),
        "other_core",
        [partial, jax.ShapeDtypeStruct((half, queries, M), bf16)],
        "vvvvv",
        queried,
        spread,
        *columns,
        scratch_shapes=[pltpu.VMEM((queries, half * LANES), f32)],
    )
    mine = call(
        functools.partial(own_core_kernel, turns),
        "own_core",
        partial,
        "vvvvv",
        queried,
        windows,
        *columns,
        flops=5 * 10**8,
    )
    narrow, column = call(
        functools.partial(own_minima_kernel, channels),
        "own_minima",
        [jax.ShapeDtypeStruct((queries, LANES), f32), jax.ShapeDtypeStruct((1, seg_len), f32)],
        "vvvv",
        mine,
        exchanged(theirs, 1),
        banned,
        beyond,
    )
    rows = call(
        functools.partial(chip_minima_kernel, turns, channels),
        "chip_minima",
        jax.ShapeDtypeStruct((turns, QB), f32),
        "vvvv",
        theirs,
        exchanged(mine, 1),
        banned,
        narrow,
    )

    crossed = [[mask + 1 for mask in (others[0], *reversed(others[1:]))] for others in rounds]
    for others in [[3], *crossed]:
        rows = functools.reduce(jnp.minimum, [exchanged(rows, mask) for mask in others], rows)
    return (rows, column.reshape(seg_len))


def solution(mesh):
    return jax.shard_map(
        shards,
        mesh=mesh,
        in_specs=(P(None, ("grp", "col")), P(None, ("grp", "col")), P("grp"), P("grp"), P("grp")),
        out_specs=(P("grp", None), P(("grp", "col"))),
        check_vma=False,
    )
```
